32 devices in a mesh: row: 4 (over z), col: 8 (over y, x, core).
Axes of the slice: x: 2, y: 2, z: 4, core: 2. Of those that a mesh axis runs over, the one named last changes fastest.
Arguments:
- matrix: float32 [2048, 2048], P('row', 'col'), may hold values from -40 to 40, as said below
Outputs:
- updated: float32 [2048, 2048], P('row', 'col')
- reflectors: float32 [8, 2048], P(None, 'row')
- images: float32 [8, 2048], P(None, 'row')
- subdiag: float32 [8], replicated
The draws below stay inside these ranges and needn't reach their ends.
Inputs may be any that keep to these rules, and one draw needn't show every extreme that they name: matrix holds a symmetric matrix of order 2048 in the stored order of the first step.
All inputs are finite; a program needn't handle non-finite values.
Results may differ from the reference program's by a relative error of at most 0.0075.
Values sent between devices are 32-bit elements; how exact they have to be, the bound alone decides.
No kernel may reach another device: no remote copies, remote signals or barrier semaphores. Data moves between devices by JAX's collectives and lax.ppermute only.
A program may use at most 64 MiB of HBM per device.

```python
import jax
import jax.numpy as jnp
from jax import lax

ROWS_DEV = 512
TILE = 128
PANEL = 8
GRID_ROWS = 4
GRID_COLS = 8
ORDER = 2048
COLS_DEV = 256


def global_of_drawn(local_count, groups, total):
    stored = jnp.arange(total, dtype=jnp.int32)
    group = stored // local_count
    within = stored % local_count
    return (within // TILE * groups + group) * TILE + within % TILE


def draw_matrix(key, part):
    total = ORDER
    raw = jax.random.normal(key, (total, total), jnp.float32)
    symmetric = (raw + jnp.transpose(raw)) * 0.70710678
    rows = global_of_drawn(ROWS_DEV, total // ROWS_DEV, total)
    cols = global_of_drawn(COLS_DEV, total // COLS_DEV, total)
    return jnp.take(jnp.take(symmetric, rows, axis=0), cols, axis=1).astype(jnp.float32)


def setup_inputs(seed: int = 0) -> dict:
    arg_keys = jax.random.split(jax.random.key(seed), 2)
    matrix = draw_matrix(jax.random.fold_in(arg_keys[1], 71), 0)
    return dict(matrix=matrix)


def global_of(local_count, groups, total):
    stored = jnp.arange(total, dtype=jnp.int32)
    group = stored // local_count
    within = stored % local_count
    return (within // TILE * groups + group) * TILE + within % TILE

def stored_of(local_count, groups, total):
    position = jnp.arange(total, dtype=jnp.int32)
    block = position // TILE
    offset = position % TILE
    return block % groups * local_count + block // groups * TILE + offset

def reference(matrix):
    highest = lax.Precision.HIGHEST
    row_global = global_of(ROWS_DEV, GRID_ROWS, ORDER)
    col_global = global_of(COLS_DEV, GRID_COLS, ORDER)
    full = jnp.take(matrix, stored_of(ROWS_DEV, GRID_ROWS, ORDER), axis=0)
    full = jnp.take(full, stored_of(COLS_DEV, GRID_COLS, ORDER), axis=1)
    positions = jnp.arange(ORDER, dtype=jnp.int32)
    refl = jnp.zeros((PANEL, ORDER), jnp.float32)
    images = jnp.zeros((PANEL, ORDER), jnp.float32)
    subdiag_list = []
    for panel_col in range(PANEL):
        column = full[:, panel_col] - jnp.dot(images[:, panel_col], refl, precision=highest) - jnp.dot(refl[:, panel_col], images, precision=highest)
        tail_mask = positions > panel_col + 1
        first_mask = positions == panel_col + 1
        leading = column[panel_col + 1]
        tail_vals = jnp.where(tail_mask, column, jnp.float32(0.0))
        squares = jnp.sum(tail_vals * tail_vals)
        radius = jnp.sqrt(leading * leading + squares)
        denominator = leading + radius
        scaling = denominator / radius
        reflector = jnp.where(tail_mask, column / denominator, jnp.where(first_mask, jnp.float32(1.0), jnp.float32(0.0)))
        product = jnp.dot(full, reflector, precision=highest)
        v_proj = jnp.dot(refl, reflector, precision=highest)
        w_proj = jnp.dot(images, reflector, precision=highest)
        image = scaling * (product - jnp.dot(w_proj, refl, precision=highest) - jnp.dot(v_proj, images, precision=highest))
        adjust = -0.5 * scaling * jnp.sum(image * reflector)
        image = image + adjust * reflector
        refl = refl.at[panel_col].set(reflector)
        images = images.at[panel_col].set(image)
        subdiag_list.append(-radius)
    left = jnp.concatenate([refl, images], axis=0)
    right = jnp.concatenate([images, refl], axis=0)
    updated = full - jnp.dot(jnp.transpose(left), right, precision=highest)
    updated = jnp.take(jnp.take(updated, row_global, axis=0), col_global, axis=1)
    return (updated, jnp.take(refl, row_global, axis=1), jnp.take(images, row_global, axis=1), jnp.stack(subdiag_list))
```

```python
import jax
import jax.numpy as jnp
from jax import lax
from jax.sharding import PartitionSpec as P

TILE = 128
PANEL = 8
AXES = ("row", "col")


def everywhere(value):
    row_count, col_count = lax.axis_size("row"), lax.axis_size("col")
    spread = jnp.broadcast_to(value[None], (row_count * col_count,) + value.shape)
    got = lax.all_to_all(spread, AXES, 0, 0, tiled=False)
    return got.reshape((row_count, col_count) + value.shape)


def per_device(matrix):
    highest = lax.Precision.HIGHEST
    local_rows, local_cols = matrix.shape
    row_count, col_count = lax.axis_size("row"), lax.axis_size("col")
    grid_row, grid_col = lax.axis_index("row"), lax.axis_index("col")
    row_tiles, col_tiles = local_rows // TILE, local_cols // TILE
    order = local_rows * row_count
    position = jnp.arange(order, dtype=jnp.int32)

    def my_rows(vectors):
        shaped = vectors.reshape(vectors.shape[:-1] + (row_tiles, row_count, TILE))
        picked = lax.dynamic_index_in_dim(shaped, grid_row, axis=shaped.ndim - 2, keepdims=False)
        return picked.reshape(vectors.shape[:-1] + (local_rows,))

    def my_cols(vectors):
        shaped = vectors.reshape(vectors.shape[:-1] + (col_tiles, col_count, TILE))
        picked = lax.dynamic_index_in_dim(shaped, grid_col, axis=shaped.ndim - 2, keepdims=False)
        return picked.reshape(vectors.shape[:-1] + (local_cols,))

    def global_cols(pieces):
        shaped = pieces.reshape(pieces.shape[:-1] + (col_tiles, TILE))
        return jnp.moveaxis(shaped, 0, -2).reshape(pieces.shape[1:-1] + (order,))

    panel = global_cols(everywhere(matrix[:PANEL])[0])
    refl = jnp.zeros((PANEL, order), jnp.float32)
    images = jnp.zeros((PANEL, order), jnp.float32)
    subdiag_list = []
    for j in range(PANEL):
        column = panel[j]
        for k in range(j):
            column = column - images[k, j] * refl[k] - refl[k, j] * images[k]
        leading = column[j + 1]
        tail = jnp.where(position > j + 1, column, 0.0)
        radius = jnp.sqrt(leading * leading + jnp.sum(tail * tail))
        denominator = leading + radius
        scaling = denominator / radius
        reflector = jnp.where(position == j + 1, 1.0, tail / denominator)
        partial = jnp.sum(matrix * my_rows(reflector)[:, None], axis=0)
        product = global_cols(jnp.sum(everywhere(partial), axis=0))
        refl_proj = jnp.sum(refl * reflector, axis=1)
        image_proj = jnp.sum(images * reflector, axis=1)
        image = product
        for k in range(j):
            image = image - image_proj[k] * refl[k] - refl_proj[k] * images[k]
        image = scaling * image
        image = image - (0.5 * scaling * jnp.sum(image * reflector)) * reflector
        refl = refl.at[j].set(reflector)
        images = images.at[j].set(image)
        subdiag_list.append(-radius)
    refl_rows, image_rows = my_rows(refl), my_rows(images)
    updated = (
        matrix
        - jnp.dot(jnp.transpose(refl_rows), my_cols(images), precision=highest)
        - jnp.dot(jnp.transpose(image_rows), my_cols(refl), precision=highest)
    )
    return (updated, refl_rows, image_rows, jnp.stack(subdiag_list))


def solution(mesh):
    return jax.shard_map(
        per_device,
        mesh=mesh,
        in_specs=(P("row", "col"),),
        out_specs=(P("row", "col"), P(None, "row"), P(None, "row"), P()),
        check_vma=False,
    )
```

```python
import jax
import jax.numpy as jnp
from jax import lax
from jax.experimental import pallas as pl
from jax.experimental.pallas import tpu as pltpu
from jax.sharding import PartitionSpec as P

TILE = 128
PANEL = 8
AXES = ("row", "col")
ROWS, COLS = 4, 8
BLOCKS = 16
HALF = BLOCKS // 2
LANES8 = TILE // 8


def everywhere(value):
    row_count, col_count = lax.axis_size("row"), lax.axis_size("col")
    spread = jnp.broadcast_to(value[None], (row_count * col_count,) + value.shape)
    got = lax.all_to_all(spread, AXES, 0, 0, tiled=False)
    return got.reshape((row_count, col_count) + value.shape)


def distributed(matrix):
    highest = lax.Precision.HIGHEST
    local_rows, local_cols = matrix.shape
    row_count, col_count = lax.axis_size("row"), lax.axis_size("col")
    grid_row, grid_col = lax.axis_index("row"), lax.axis_index("col")
    row_tiles, col_tiles = local_rows // TILE, local_cols // TILE
    order = local_rows * row_count
    position = jnp.arange(order, dtype=jnp.int32)

    def my_rows(vectors):
        shaped = vectors.reshape(vectors.shape[:-1] + (row_tiles, row_count, TILE))
        picked = lax.dynamic_index_in_dim(shaped, grid_row, axis=shaped.ndim - 2, keepdims=False)
        return picked.reshape(vectors.shape[:-1] + (local_rows,))

    def my_cols(vectors):
        shaped = vectors.reshape(vectors.shape[:-1] + (col_tiles, col_count, TILE))
        picked = lax.dynamic_index_in_dim(shaped, grid_col, axis=shaped.ndim - 2, keepdims=False)
        return picked.reshape(vectors.shape[:-1] + (local_cols,))

    def global_cols(pieces):
        shaped = pieces.reshape(pieces.shape[:-1] + (col_tiles, TILE))
        return jnp.moveaxis(shaped, 0, -2).reshape(pieces.shape[1:-1] + (order,))

    panel = global_cols(everywhere(matrix[:PANEL])[0])
    refl = jnp.zeros((PANEL, order), jnp.float32)
    images = jnp.zeros((PANEL, order), jnp.float32)
    subdiag_list = []
    for j in range(PANEL):
        column = panel[j]
        for k in range(j):
            column = column - images[k, j] * refl[k] - refl[k, j] * images[k]
        leading = column[j + 1]
        tail = jnp.where(position > j + 1, column, 0.0)
        radius = jnp.sqrt(leading * leading + jnp.sum(tail * tail))
        denominator = leading + radius
        scaling = denominator / radius
        reflector = jnp.where(position == j + 1, 1.0, tail / denominator)
        partial = jnp.sum(matrix * my_rows(reflector)[:, None], axis=0)
        product = global_cols(jnp.sum(everywhere(partial), axis=0))
        refl_proj = jnp.sum(refl * reflector, axis=1)
        image_proj = jnp.sum(images * reflector, axis=1)
        image = product
        for k in range(j):
            image = image - image_proj[k] * refl[k] - refl_proj[k] * images[k]
        image = scaling * image
        image = image - (0.5 * scaling * jnp.sum(image * reflector)) * reflector
        refl = refl.at[j].set(reflector)
        images = images.at[j].set(image)
        subdiag_list.append(-radius)
    refl_rows, image_rows = my_rows(refl), my_rows(images)
    updated = (
        matrix
        - jnp.dot(jnp.transpose(refl_rows), my_cols(images), precision=highest)
        - jnp.dot(jnp.transpose(image_rows), my_cols(refl), precision=highest)
    )
    return (updated, refl_rows, image_rows, jnp.stack(subdiag_list))


def pick_kernel(index, matrix, block, block_extra):
    r, c = index[0], index[1]
    d = lax.rem(r - c + COLS, ROWS)
    first = (c + d) // ROWS

    def tile(k, m):
        start = pl.multiple_of(lax.rem(k, ROWS) * TILE, TILE)
        return matrix[pl.ds(start, TILE), m * TILE : (m + 1) * TILE]

    for m in range(2):
        for s in range(2):
            value = tile(first + 2 * m + s, m)
            block[2 * m + s] = value
            block_extra[2 * m + s] = value
    block_extra[4] = jnp.where(d == 0, tile(first + 2, 0), 0.0)


def pick(index, matrix):
    vmem = pl.BlockSpec(memory_space=pltpu.VMEM)
    return pl.pallas_call(
        pick_kernel,
        out_shape=(
            jax.ShapeDtypeStruct((4, TILE, TILE), jnp.float32),
            jax.ShapeDtypeStruct((5, TILE, TILE), jnp.float32),
        ),
        in_specs=[pl.BlockSpec(memory_space=pltpu.SMEM), vmem],
        out_specs=(vmem, vmem),
        compiler_params=pltpu.CompilerParams(vmem_limit_bytes=4 * 1024 * 1024),
    )(index, matrix)


def involution(move):
    return [(r * COLS + c, move(r, c)[0] * COLS + move(r, c)[1]) for r in range(ROWS) for c in range(COLS)]


TO_CORE = involution(lambda r, c: (r, c ^ 1))
SIDE_A = involution(lambda r, c: (r, c ^ 2 if c % 2 == 0 else c ^ 4))
SIDE_B = involution(lambda r, c: (r, c ^ 4 if c % 2 == 0 else c ^ 2))
OUTER = involution(lambda r, c: (r ^ 1, c))
MIDDLE = [(r * COLS + c, (3 - r) * COLS + c) for r in (1, 2) for c in range(COLS)]


def send(value, pairs):
    return lax.ppermute(value, AXES, pairs)


GROUPS = ((0, 1, 2, 3), (4, 5, 8, 10), (6, 9, 12), (7, 11, 13, 14, 15))


def gather(a, a5):
    ua, ma, b, c = send(a5, OUTER), send(a5, MIDDLE), send(a, SIDE_A), send(a, SIDE_B)
    e, ub, na, mc = send(b, SIDE_B), send(b, OUTER), send(ua, MIDDLE), send(ma, SIDE_B)
    uc, mb = send(c, OUTER), send(b, MIDDLE)
    na = jnp.concatenate([na[:4], (a5[4:] + ua[4:]) + (ma[4:] + na[4:])])
    nb, nc = send(na, SIDE_A), send(na, SIDE_B)
    ue, me, ne = send(e, OUTER), send(mb, SIDE_B), send(nb, SIDE_B)
    own = (a, b, c, e, ua, ub, uc, ue, ma, mb, mc, me, na, nb, nc, ne)
    return own, tuple(send(jnp.concatenate([own[i] for i in group]), TO_CORE) for group in GROUPS)


def tile_place(big_r, delta):
    big_c = (big_r - delta) % BLOCKS
    return big_c % COLS, delta % 4, 2 * (big_c // COLS) + delta // 4


def panel_kernel(index, *refs):
    own = refs[:16]
    others = refs[16 : 16 + len(GROUPS)]
    out, store, extra_store, v_all, w_all, p_all, rows, acc, sems = refs[16 + len(GROUPS) :]
    r, c = index[0], index[1]

    def source_of(number, col):
        z, side = number // 4, number % 4
        row = (r, r ^ 1, 3 - r, (3 - r) ^ 1)[z]
        even = lax.rem(col, 2) == 0
        flip = (0, jnp.where(even, 2, 4), jnp.where(even, 4, 2), 6)[side]
        return row, col ^ flip

    copies = []

    def load(source, start, number, col):
        row, from_col = source_of(number, col)
        d = lax.rem(row - from_col + COLS, ROWS)
        copies.append(
            pltpu.make_async_copy(source.at[pl.ds(start, 4)], store.at[from_col, d], sems.at[len(copies)])
        )
        if number >= 12:
            copies.append(
                pltpu.make_async_copy(source.at[start + 4], extra_store.at[from_col], sems.at[len(copies)])
            )

    for number in range(16):
        load(own[number], 0, number, c)
    for ref, group in zip(others, GROUPS):
        start = 0
        for number in group:
            load(ref, start, number, c ^ 1)
            start += own[number].shape[0]
    for copy in copies:
        copy.start()
    for copy in copies:
        copy.wait()

    def tile(big_r, delta):
        if delta == HALF:
            return extra_store[big_r - HALF]
        return store[tile_place(big_r, delta)]

    block_row = lax.broadcasted_iota(jnp.int32, (BLOCKS, TILE), 0)
    lane = lax.broadcasted_iota(jnp.int32, (BLOCKS, TILE), 1)
    position = block_row * TILE + lane
    on_diagonal = lax.broadcasted_iota(jnp.int32, (PANEL, TILE), 0) == lax.broadcasted_iota(
        jnp.int32, (PANEL, TILE), 1
    )
    which = lax.broadcasted_iota(jnp.int32, (BLOCKS, PANEL, TILE), 1)
    which_sub = lax.broadcasted_iota(jnp.int32, (PANEL, TILE), 0)

    def total(x):
        return jnp.sum(jnp.sum(x, axis=0, keepdims=True), axis=1, keepdims=True)

    for big_c in range(BLOCKS):
        delta = -big_c % BLOCKS
        if delta < HALF:
            rows[big_c] = tile(0, delta)[:16]
        else:
            rows[big_c] = jnp.transpose(tile(big_c, big_c))[:16]
    v_all[...] = jnp.zeros_like(v_all)
    w_all[...] = jnp.zeros_like(w_all)
    p_all[...] = rows[:, :PANEL, :]
    out[BLOCKS] = jnp.zeros((2 * PANEL, TILE), jnp.float32)

    def multiply(vector):
        for big_c in range(BLOCKS):
            acc[big_c] = jnp.zeros((8, TILE), jnp.float32)
        sums = []
        for big_r in range(BLOCKS):
            down = jnp.transpose(jnp.broadcast_to(vector[big_r : big_r + 1], (TILE, TILE)))
            across = None
            for delta in range(HALF + 1):
                if delta == HALF and big_r < HALF:
                    continue
                big_c = (big_r - delta) % BLOCKS
                t = tile(big_r, delta)
                acc[big_c] += jnp.sum((t * down).reshape(LANES8, 8, TILE), axis=0)
                if delta > 0:
                    part = t * vector[big_c : big_c + 1]
                    across = part if across is None else across + part
            sums.append(jnp.sum(jnp.transpose(across).reshape(LANES8, 8, TILE), axis=0))
        for big_r in range(BLOCKS):
            acc[big_r] += sums[big_r]
        return jnp.sum(acc[...], axis=1)

    def step(j, column):
        first = position == j + 1
        tail = jnp.where(position > j + 1, column, 0.0)
        tail_product = multiply(tail)
        leading = total(jnp.where(first, column, 0.0))
        squares = total(tail * tail)
        radius = jnp.sqrt(leading * leading + squares)
        denominator = leading + radius
        scaling = denominator / radius
        inverse = 1.0 / denominator
        v = jnp.where(first, 1.0, tail * inverse)
        v3 = v[:, None, :]
        refl, images = v_all[...], w_all[...]
        refl_proj = jnp.sum(jnp.sum(refl * v3, axis=0), axis=1, keepdims=True)
        image_proj = jnp.sum(jnp.sum(images * v3, axis=0), axis=1, keepdims=True)
        correction = jnp.sum(refl * image_proj[None] + images * refl_proj[None], axis=1)
        v_correction = 2.0 * jnp.sum(refl_proj * image_proj, axis=0, keepdims=True)
        product = tail_product * inverse + rows[:, pl.ds(j + 1, 1), :].reshape(BLOCKS, TILE)
        inner = scaling * (total(v * product) - v_correction)
        w = scaling * (product - correction) - (0.5 * scaling * inner) * v
        w3 = w[:, None, :]
        v_heads = jnp.sum(jnp.where(on_diagonal, v[0:1], 0.0), axis=1, keepdims=True)
        w_heads = jnp.sum(jnp.where(on_diagonal, w[0:1], 0.0), axis=1, keepdims=True)
        panel = p_all[...] - w_heads[None] * v3 - v_heads[None] * w3
        p_all[...] = panel
        v_all[...] = jnp.where(which == j, v3, refl)
        w_all[...] = jnp.where(which == j, w3, images)
        out[BLOCKS, :PANEL, :] = jnp.where(which_sub == j, -radius, out[BLOCKS, :PANEL, :])
        return jnp.sum(jnp.where(which == j + 1, panel, 0.0), axis=1)

    lax.fori_loop(0, PANEL, step, rows[:, 0, :])
    out[:BLOCKS, :PANEL, :] = v_all[...]
    out[:BLOCKS, PANEL:, :] = w_all[...]


def reduce_panel(index, own, others):
    held = pl.BlockSpec(memory_space=pltpu.VMEM)
    vmem = pl.BlockSpec(memory_space=pltpu.VMEM)
    return pl.pallas_call(
        panel_kernel,
        out_shape=jax.ShapeDtypeStruct((BLOCKS + 1, 2 * PANEL, TILE), jnp.float32),
        in_specs=[pl.BlockSpec(memory_space=pltpu.SMEM)] + [held] * (16 + len(others)),
        out_specs=vmem,
        scratch_shapes=[
            pltpu.VMEM((COLS, ROWS, 4, TILE, TILE), jnp.float32),
            pltpu.VMEM((HALF, TILE, TILE), jnp.float32),
            pltpu.VMEM((BLOCKS, PANEL, TILE), jnp.float32),
            pltpu.VMEM((BLOCKS, PANEL, TILE), jnp.float32),
            pltpu.VMEM((BLOCKS, PANEL, TILE), jnp.float32),
            pltpu.VMEM((BLOCKS, 2 * PANEL, TILE), jnp.float32),
            pltpu.VMEM((BLOCKS, 8, TILE), jnp.float32),
            pltpu.SemaphoreType.DMA((40,)),
        ],
        compiler_params=pltpu.CompilerParams(vmem_limit_bytes=24 * 1024 * 1024),
    )(index, *own, *others)


def update_kernel(index, matrix, mine, theirs, updated, refl_rows, image_rows, subdiag, held):
    r, c = index[0], index[1]

    @pl.when(jnp.logical_or(r == 1, r == 2))
    def _():
        held[...] = mine[...]

    @pl.when(jnp.logical_or(r == 0, r == 3))
    def _():
        held[...] = theirs[...]

    right = []
    for m in range(2):
        both = held[m * COLS + c]
        right.append(jnp.concatenate([both[PANEL:], both[:PANEL]], axis=0))
    right = jnp.concatenate(right, axis=1)
    for k in range(4):
        left = held[k * ROWS + r]
        span = slice(k * TILE, (k + 1) * TILE)
        updated[span, :] = matrix[span, :] - lax.dot_general(
            left,
            right,
            (((0,), (0,)), ((), ())),
            precision=lax.Precision.HIGHEST,
            preferred_element_type=jnp.float32,
        )
        refl_rows[:, span] = left[:PANEL]
        image_rows[:, span] = left[PANEL:]
    subdiag[...] = held[BLOCKS, :PANEL, :]


def finish(index, matrix, mine, theirs):
    vmem = pl.BlockSpec(memory_space=pltpu.VMEM)
    rows, _ = matrix.shape
    return pl.pallas_call(
        update_kernel,
        out_shape=(
            jax.ShapeDtypeStruct(matrix.shape, jnp.float32),
            jax.ShapeDtypeStruct((PANEL, rows), jnp.float32),
            jax.ShapeDtypeStruct((PANEL, rows), jnp.float32),
            jax.ShapeDtypeStruct((PANEL, TILE), jnp.float32),
        ),
        in_specs=[pl.BlockSpec(memory_space=pltpu.SMEM), vmem, vmem, vmem],
        out_specs=(vmem,) * 4,
        scratch_shapes=[pltpu.VMEM(mine.shape, jnp.float32)],
        compiler_params=pltpu.CompilerParams(vmem_limit_bytes=6 * 1024 * 1024),
    )(index, matrix, mine, theirs)


def gathered(matrix):
    index = jnp.stack([lax.axis_index("row"), lax.axis_index("col")]).astype(jnp.int32)
    own, others = gather(*pick(index, matrix))
    mine = reduce_panel(index, own, others)
    theirs = send(mine, OUTER)
    updated, refl_rows, image_rows, subdiag = finish(index, matrix, mine, theirs)
    return updated, refl_rows, image_rows, subdiag[:, 0]


def per_device(matrix):
    grid = (lax.axis_size("row"), lax.axis_size("col"))
    if grid == (ROWS, COLS) and matrix.shape == (BLOCKS // ROWS * TILE, BLOCKS // COLS * TILE):
        return gathered(matrix)
    return distributed(matrix)


def solution(mesh):
    return jax.shard_map(
        per_device,
        mesh=mesh,
        in_specs=(P("row", "col"),),
        out_specs=(P("row", "col"), P(None, "row"), P(None, "row"), P()),
        check_vma=False,
    )
```

```python
import jax
import jax.numpy as jnp
from jax import lax
from jax.experimental import pallas as pl
from jax.experimental.pallas import tpu as pltpu
from jax.sharding import PartitionSpec as P

TILE = 128
PANEL = 8
AXES = ("row", "col")
ROWS, COLS = 4, 8
BLOCKS = 16
HALF = BLOCKS // 2
LANES8 = TILE // 8


def everywhere(value):
    row_count, col_count = lax.axis_size("row"), lax.axis_size("col")
    spread = jnp.broadcast_to(value[None], (row_count * col_count,) + value.shape)
    got = lax.all_to_all(spread, AXES, 0, 0, tiled=False)
    return got.reshape((row_count, col_count) + value.shape)


def distributed(matrix):
    highest = lax.Precision.HIGHEST
    local_rows, local_cols = matrix.shape
    row_count, col_count = lax.axis_size("row"), lax.axis_size("col")
    grid_row, grid_col = lax.axis_index("row"), lax.axis_index("col")
    row_tiles, col_tiles = local_rows // TILE, local_cols // TILE
    order = local_rows * row_count
    position = jnp.arange(order, dtype=jnp.int32)

    def my_rows(vectors):
        shaped = vectors.reshape(vectors.shape[:-1] + (row_tiles, row_count, TILE))
        picked = lax.dynamic_index_in_dim(shaped, grid_row, axis=shaped.ndim - 2, keepdims=False)
        return picked.reshape(vectors.shape[:-1] + (local_rows,))

    def my_cols(vectors):
        shaped = vectors.reshape(vectors.shape[:-1] + (col_tiles, col_count, TILE))
        picked = lax.dynamic_index_in_dim(shaped, grid_col, axis=shaped.ndim - 2, keepdims=False)
        return picked.reshape(vectors.shape[:-1] + (local_cols,))

    def global_cols(pieces):
        shaped = pieces.reshape(pieces.shape[:-1] + (col_tiles, TILE))
        return jnp.moveaxis(shaped, 0, -2).reshape(pieces.shape[1:-1] + (order,))

    panel = global_cols(everywhere(matrix[:PANEL])[0])
    refl = jnp.zeros((PANEL, order), jnp.float32)
    images = jnp.zeros((PANEL, order), jnp.float32)
    subdiag_list = []
    for j in range(PANEL):
        column = panel[j]
        for k in range(j):
            column = column - images[k, j] * refl[k] - refl[k, j] * images[k]
        leading = column[j + 1]
        tail = jnp.where(position > j + 1, column, 0.0)
        radius = jnp.sqrt(leading * leading + jnp.sum(tail * tail))
        denominator = leading + radius
        scaling = denominator / radius
        reflector = jnp.where(position == j + 1, 1.0, tail / denominator)
        partial = jnp.sum(matrix * my_rows(reflector)[:, None], axis=0)
        product = global_cols(jnp.sum(everywhere(partial), axis=0))
        refl_proj = jnp.sum(refl * reflector, axis=1)
        image_proj = jnp.sum(images * reflector, axis=1)
        image = product
        for k in range(j):
            image = image - image_proj[k] * refl[k] - refl_proj[k] * images[k]
        image = scaling * image
        image = image - (0.5 * scaling * jnp.sum(image * reflector)) * reflector
        refl = refl.at[j].set(reflector)
        images = images.at[j].set(image)
        subdiag_list.append(-radius)
    refl_rows, image_rows = my_rows(refl), my_rows(images)
    updated = (
        matrix
        - jnp.dot(jnp.transpose(refl_rows), my_cols(images), precision=highest)
        - jnp.dot(jnp.transpose(image_rows), my_cols(refl), precision=highest)
    )
    return (updated, refl_rows, image_rows, jnp.stack(subdiag_list))


def pick_kernel(index, matrix, block, block_extra):
    r, c = index[0], index[1]
    d = lax.rem(r - c + COLS, ROWS)
    first = (c + d) // ROWS

    def tile(k, m):
        start = pl.multiple_of(lax.rem(k, ROWS) * TILE, TILE)
        return matrix[pl.ds(start, TILE), m * TILE : (m + 1) * TILE]

    for m in range(2):
        for s in range(2):
            value = tile(first + 2 * m + s, m)
            block[2 * m + s] = value
            block_extra[2 * m + s] = value
    block_extra[4] = jnp.where(d == 0, tile(first + 2, 0), 0.0)


def pick(index, matrix):
    vmem = pl.BlockSpec(memory_space=pltpu.VMEM)
    return pl.pallas_call(
        pick_kernel,
        out_shape=(
            jax.ShapeDtypeStruct((4, TILE, TILE), jnp.float32),
            jax.ShapeDtypeStruct((5, TILE, TILE), jnp.float32),
        ),
        in_specs=[pl.BlockSpec(memory_space=pltpu.SMEM), vmem],
        out_specs=(vmem, vmem),
        compiler_params=pltpu.CompilerParams(vmem_limit_bytes=4 * 1024 * 1024),
    )(index, matrix)


def involution(move):
    return [(r * COLS + c, move(r, c)[0] * COLS + move(r, c)[1]) for r in range(ROWS) for c in range(COLS)]


TO_CORE = involution(lambda r, c: (r, c ^ 1))
SIDE_A = involution(lambda r, c: (r, c ^ 2 if c % 2 == 0 else c ^ 4))
SIDE_B = involution(lambda r, c: (r, c ^ 4 if c % 2 == 0 else c ^ 2))
OUTER = involution(lambda r, c: (r ^ 1, c))
MIDDLE = involution(lambda r, c: (3 - r, c) if r in (1, 2) else (r, c ^ 1))


def send(value, pairs):
    return lax.ppermute(value, AXES, pairs)


GROUPS = ((0, 1, 2, 4, 8), (3, 6, 10, 5, 9, 12), (14, 7, 11, 13), (15, 16))


def gather(a, a5):
    b = send(a, SIDE_A)
    ua = send(a5, OUTER)
    ma = send(a5, MIDDLE)
    c = send(a, SIDE_B)
    first_b = send(jnp.concatenate([b, ua[:4], ma[:4]]), SIDE_B)
    na = send(ua, MIDDLE)
    mb = send(ma[:4], SIDE_A)
    ub = send(b, OUTER)
    g0 = send(jnp.concatenate([a, b, c, ua, ma]), TO_CORE)
    e = first_b[:4]
    uc = first_b[4:8]
    mc = first_b[8:]
    tile = (a5[4:] + ua[4:]) + (ma[4:] + na[4:])
    nb = send(ub, MIDDLE)
    tile_a = send(tile, SIDE_A)
    second_b = send(jnp.concatenate([na[:4], tile, ub, mb]), SIDE_B)
    g1 = send(jnp.concatenate([e, uc, mc, ub, mb, na]), TO_CORE)
    nc = second_b[:4]
    tile_b = second_b[4:5]
    ue = second_b[5:9]
    me = second_b[9:]
    third_b = send(jnp.concatenate([nb, tile_a]), SIDE_B)
    ne = third_b[:4]
    tiles = jnp.concatenate([tile, tile_a, tile_b, third_b[4:]])
    g2 = send(jnp.concatenate([nc, ue, me, nb]), TO_CORE)
    g3 = send(jnp.concatenate([ne, tiles]), TO_CORE)
    own = (a, b, c, e, ua, ub, uc, ue, ma, mb, mc, me, na, nb, nc, ne, tiles)
    return own, (g0, g1, g2, g3)


def tile_place(big_r, delta):
    big_c = (big_r - delta) % BLOCKS
    return big_c % COLS, delta % 4, 2 * (big_c // COLS) + delta // 4


def panel_kernel(index, *refs):
    own = refs[:17]
    others = refs[17 : 17 + len(GROUPS)]
    for_me, for_next, store, extra_store, v_all, w_all, p_all, rows, acc, radii, sems = refs[17 + len(GROUPS) :]
    r, c = index[0], index[1]

    def source_of(number, col):
        z, side = number // 4, number % 4
        row = (r, r ^ 1, 3 - r, (3 - r) ^ 1)[z]
        even = lax.rem(col, 2) == 0
        flip = (0, jnp.where(even, 2, 4), jnp.where(even, 4, 2), 6)[side]
        return row, col ^ flip

    copies = []

    def load(source, start, number, col):
        row, from_col = source_of(number, col)
        d = lax.rem(row - from_col + COLS, ROWS)
        copies.append(
            pltpu.make_async_copy(source.at[pl.ds(start, 4)], store.at[from_col, d], sems.at[len(copies)])
        )

    def load_extra(source, start, col):
        for side in range(4):
            _, from_col = source_of(side, col)
            copies.append(
                pltpu.make_async_copy(source.at[start + side], extra_store.at[from_col], sems.at[len(copies)])
            )

    for number in range(16):
        load(own[number], 0, number, c)
    load_extra(own[16], 0, c)
    for ref, group in zip(others, GROUPS):
        start = 0
        for number in group:
            if number == 16:
                load_extra(ref, start, c ^ 1)
            else:
                load(ref, start, number, c ^ 1)
            start += own[number].shape[0]
    for copy in copies:
        copy.start()
    for copy in copies:
        copy.wait()

    def tile(big_r, delta):
        if delta == HALF:
            return extra_store[big_r - HALF]
        return store[tile_place(big_r, delta)]

    block_row = lax.broadcasted_iota(jnp.int32, (BLOCKS, TILE), 0)
    lane = lax.broadcasted_iota(jnp.int32, (BLOCKS, TILE), 1)
    position = block_row * TILE + lane
    on_diagonal = lax.broadcasted_iota(jnp.int32, (PANEL, TILE), 0) == lax.broadcasted_iota(
        jnp.int32, (PANEL, TILE), 1
    )
    which = lax.broadcasted_iota(jnp.int32, (BLOCKS, PANEL, TILE), 1)
    which_sub = lax.broadcasted_iota(jnp.int32, (1, TILE), 1)

    def total(x):
        return jnp.sum(jnp.sum(x, axis=0, keepdims=True), axis=1, keepdims=True)

    for big_c in range(BLOCKS):
        delta = -big_c % BLOCKS
        if delta < HALF:
            rows[big_c] = tile(0, delta)[:16]
        else:
            rows[big_c] = jnp.transpose(tile(big_c, big_c))[:16]
    v_all[...] = jnp.zeros_like(v_all)
    w_all[...] = jnp.zeros_like(w_all)
    p_all[...] = rows[:, :PANEL, :]
    radii[...] = jnp.zeros_like(radii)

    def multiply(vector):
        for big_c in range(BLOCKS):
            acc[big_c] = jnp.zeros((8, TILE), jnp.float32)
        sums = []
        for big_r in range(BLOCKS):
            down = jnp.transpose(jnp.broadcast_to(vector[big_r : big_r + 1], (TILE, TILE)))
            across = None
            for delta in range(HALF + 1):
                if delta == HALF and big_r < HALF:
                    continue
                big_c = (big_r - delta) % BLOCKS
                t = tile(big_r, delta)
                acc[big_c] += jnp.sum((t * down).reshape(LANES8, 8, TILE), axis=0)
                if delta > 0:
                    part = t * vector[big_c : big_c + 1]
                    across = part if across is None else across + part
            sums.append(jnp.sum(jnp.transpose(across).reshape(LANES8, 8, TILE), axis=0))
        for big_r in range(BLOCKS):
            acc[big_r] += sums[big_r]
        return jnp.sum(acc[...], axis=1)

    def step(j, column):
        first = position == j + 1
        tail = jnp.where(position > j + 1, column, 0.0)
        tail_product = multiply(tail)
        leading = total(jnp.where(first, column, 0.0))
        squares = total(tail * tail)
        radius = jnp.sqrt(leading * leading + squares)
        denominator = leading + radius
        scaling = denominator / radius
        inverse = 1.0 / denominator
        v = jnp.where(first, 1.0, tail * inverse)
        v3 = v[:, None, :]
        refl, images = v_all[...], w_all[...]
        refl_proj = jnp.sum(jnp.sum(refl * v3, axis=0), axis=1, keepdims=True)
        image_proj = jnp.sum(jnp.sum(images * v3, axis=0), axis=1, keepdims=True)
        correction = jnp.sum(refl * image_proj[None] + images * refl_proj[None], axis=1)
        v_correction = 2.0 * jnp.sum(refl_proj * image_proj, axis=0, keepdims=True)
        product = tail_product * inverse + rows[:, pl.ds(j + 1, 1), :].reshape(BLOCKS, TILE)
        inner = scaling * (total(v * product) - v_correction)
        w = scaling * (product - correction) - (0.5 * scaling * inner) * v
        w3 = w[:, None, :]
        v_heads = jnp.sum(jnp.where(on_diagonal, v[0:1], 0.0), axis=1, keepdims=True)
        w_heads = jnp.sum(jnp.where(on_diagonal, w[0:1], 0.0), axis=1, keepdims=True)
        panel = p_all[...] - w_heads[None] * v3 - v_heads[None] * w3
        p_all[...] = panel
        v_all[...] = jnp.where(which == j, v3, refl)
        w_all[...] = jnp.where(which == j, w3, images)
        radii[...] = jnp.where(which_sub == j, -radius, radii[...])
        return jnp.sum(jnp.where(which == j + 1, panel, 0.0), axis=1)

    lax.fori_loop(0, PANEL, step, rows[:, 0, :])
    for out, row in ((for_me, r), (for_next, r ^ 1)):
        blocks = [k * ROWS + row for k in range(4)] + [m * COLS + c for m in range(2)]
        for place, number in enumerate(blocks):
            out[place, :PANEL, :] = v_all[number]
            out[place, PANEL:, :] = w_all[number]
        out[6] = jnp.broadcast_to(radii[...], (2 * PANEL, TILE))


def reduce_panel(index, own, others):
    held = pl.BlockSpec(memory_space=pltpu.VMEM)
    vmem = pl.BlockSpec(memory_space=pltpu.VMEM)
    return pl.pallas_call(
        panel_kernel,
        out_shape=(jax.ShapeDtypeStruct((7, 2 * PANEL, TILE), jnp.float32),) * 2,
        in_specs=[pl.BlockSpec(memory_space=pltpu.SMEM)] + [held] * (17 + len(others)),
        out_specs=(vmem, vmem),
        scratch_shapes=[
            pltpu.VMEM((COLS, ROWS, 4, TILE, TILE), jnp.float32),
            pltpu.VMEM((HALF, TILE, TILE), jnp.float32),
            pltpu.VMEM((BLOCKS, PANEL, TILE), jnp.float32),
            pltpu.VMEM((BLOCKS, PANEL, TILE), jnp.float32),
            pltpu.VMEM((BLOCKS, PANEL, TILE), jnp.float32),
            pltpu.VMEM((BLOCKS, 2 * PANEL, TILE), jnp.float32),
            pltpu.VMEM((BLOCKS, 8, TILE), jnp.float32),
            pltpu.VMEM((1, TILE), jnp.float32),
            pltpu.SemaphoreType.DMA((40,)),
        ],
        compiler_params=pltpu.CompilerParams(vmem_limit_bytes=24 * 1024 * 1024),
    )(index, *own, *others)


def update_kernel(index, matrix, mine, theirs, updated, refl_rows, image_rows, subdiag, held):
    r = index[0]

    @pl.when(jnp.logical_or(r == 1, r == 2))
    def _():
        held[...] = mine[...]

    @pl.when(jnp.logical_or(r == 0, r == 3))
    def _():
        held[...] = theirs[...]

    right = []
    for m in range(2):
        both = held[4 + m]
        right.append(jnp.concatenate([both[PANEL:], both[:PANEL]], axis=0))
    right = jnp.concatenate(right, axis=1)
    for k in range(4):
        left = held[k]
        span = slice(k * TILE, (k + 1) * TILE)
        updated[span, :] = matrix[span, :] - lax.dot_general(
            left,
            right,
            (((0,), (0,)), ((), ())),
            precision=lax.Precision.HIGHEST,
            preferred_element_type=jnp.float32,
        )
        refl_rows[:, span] = left[:PANEL]
        image_rows[:, span] = left[PANEL:]
    subdiag[...] = held[6, 0, :PANEL]


def finish(index, matrix, mine, theirs):
    vmem = pl.BlockSpec(memory_space=pltpu.VMEM)
    rows, _ = matrix.shape
    return pl.pallas_call(
        update_kernel,
        out_shape=(
            jax.ShapeDtypeStruct(matrix.shape, jnp.float32),
            jax.ShapeDtypeStruct((PANEL, rows), jnp.float32),
            jax.ShapeDtypeStruct((PANEL, rows), jnp.float32),
            jax.ShapeDtypeStruct((PANEL,), jnp.float32),
        ),
        in_specs=[pl.BlockSpec(memory_space=pltpu.SMEM), vmem, vmem, vmem],
        out_specs=(vmem,) * 4,
        scratch_shapes=[pltpu.VMEM(mine.shape, jnp.float32)],
        compiler_params=pltpu.CompilerParams(vmem_limit_bytes=6 * 1024 * 1024),
    )(index, matrix, mine, theirs)


def gathered(matrix):
    index = jnp.stack([lax.axis_index("row"), lax.axis_index("col")]).astype(jnp.int32)
    own, others = gather(*pick(index, matrix))
    mine, for_next = reduce_panel(index, own, others)
    return tuple(finish(index, matrix, mine, send(for_next, OUTER)))


def per_device(matrix):
    grid = (lax.axis_size("row"), lax.axis_size("col"))
    if grid == (ROWS, COLS) and matrix.shape == (BLOCKS // ROWS * TILE, BLOCKS // COLS * TILE):
        return gathered(matrix)
    return distributed(matrix)


def solution(mesh):
    return jax.shard_map(
        per_device,
        mesh=mesh,
        in_specs=(P("row", "col"),),
        out_specs=(P("row", "col"), P(None, "row"), P(None, "row"), P()),
        check_vma=False,
    )
```

```python
import jax
import jax.numpy as jnp
from jax import lax
from jax.experimental import pallas as pl
from jax.experimental.pallas import tpu as pltpu
from jax.sharding import PartitionSpec as P

TILE = 128
PANEL = 8
AXES = ("row", "col")
ROWS, COLS = 4, 8
BLOCKS = 16
HALF = BLOCKS // 2
LANES8 = TILE // 8


def everywhere(value):
    row_count, col_count = lax.axis_size("row"), lax.axis_size("col")
    spread = jnp.broadcast_to(value[None], (row_count * col_count,) + value.shape)
    got = lax.all_to_all(spread, AXES, 0, 0, tiled=False)
    return got.reshape((row_count, col_count) + value.shape)


def distributed(matrix):
    highest = lax.Precision.HIGHEST
    local_rows, local_cols = matrix.shape
    row_count, col_count = lax.axis_size("row"), lax.axis_size("col")
    grid_row, grid_col = lax.axis_index("row"), lax.axis_index("col")
    row_tiles, col_tiles = local_rows // TILE, local_cols // TILE
    order = local_rows * row_count
    position = jnp.arange(order, dtype=jnp.int32)

    def my_rows(vectors):
        shaped = vectors.reshape(vectors.shape[:-1] + (row_tiles, row_count, TILE))
        picked = lax.dynamic_index_in_dim(shaped, grid_row, axis=shaped.ndim - 2, keepdims=False)
        return picked.reshape(vectors.shape[:-1] + (local_rows,))

    def my_cols(vectors):
        shaped = vectors.reshape(vectors.shape[:-1] + (col_tiles, col_count, TILE))
        picked = lax.dynamic_index_in_dim(shaped, grid_col, axis=shaped.ndim - 2, keepdims=False)
        return picked.reshape(vectors.shape[:-1] + (local_cols,))

    def global_cols(pieces):
        shaped = pieces.reshape(pieces.shape[:-1] + (col_tiles, TILE))
        return jnp.moveaxis(shaped, 0, -2).reshape(pieces.shape[1:-1] + (order,))

    panel = global_cols(everywhere(matrix[:PANEL])[0])
    refl = jnp.zeros((PANEL, order), jnp.float32)
    images = jnp.zeros((PANEL, order), jnp.float32)
    subdiag_list = []
    for j in range(PANEL):
        column = panel[j]
        for k in range(j):
            column = column - images[k, j] * refl[k] - refl[k, j] * images[k]
        leading = column[j + 1]
        tail = jnp.where(position > j + 1, column, 0.0)
        radius = jnp.sqrt(leading * leading + jnp.sum(tail * tail))
        denominator = leading + radius
        scaling = denominator / radius
        reflector = jnp.where(position == j + 1, 1.0, tail / denominator)
        partial = jnp.sum(matrix * my_rows(reflector)[:, None], axis=0)
        product = global_cols(jnp.sum(everywhere(partial), axis=0))
        refl_proj = jnp.sum(refl * reflector, axis=1)
        image_proj = jnp.sum(images * reflector, axis=1)
        image = product
        for k in range(j):
            image = image - image_proj[k] * refl[k] - refl_proj[k] * images[k]
        image = scaling * image
        image = image - (0.5 * scaling * jnp.sum(image * reflector)) * reflector
        refl = refl.at[j].set(reflector)
        images = images.at[j].set(image)
        subdiag_list.append(-radius)
    refl_rows, image_rows = my_rows(refl), my_rows(images)
    updated = (
        matrix
        - jnp.dot(jnp.transpose(refl_rows), my_cols(images), precision=highest)
        - jnp.dot(jnp.transpose(image_rows), my_cols(refl), precision=highest)
    )
    return (updated, refl_rows, image_rows, jnp.stack(subdiag_list))


def pick_kernel(index, matrix, block, block_extra):
    r, c = index[0], index[1]
    d = lax.rem(r - c + COLS, ROWS)
    first = (c + d) // ROWS

    def tile(k, m):
        start = pl.multiple_of(lax.rem(k, ROWS) * TILE, TILE)
        return matrix[pl.ds(start, TILE), m * TILE : (m + 1) * TILE]

    for m in range(2):
        for s in range(2):
            value = tile(first + 2 * m + s, m)
            block[2 * m + s] = value
            block_extra[2 * m + s] = value
    block_extra[4] = jnp.where(d == 0, tile(first + 2, 0), 0.0)


def pick(index, matrix):
    vmem = pl.BlockSpec(memory_space=pltpu.VMEM)
    return pl.pallas_call(
        pick_kernel,
        out_shape=(
            jax.ShapeDtypeStruct((4, TILE, TILE), jnp.float32),
            jax.ShapeDtypeStruct((5, TILE, TILE), jnp.float32),
        ),
        in_specs=[pl.BlockSpec(memory_space=pltpu.SMEM), vmem],
        out_specs=(vmem, vmem),
        compiler_params=pltpu.CompilerParams(vmem_limit_bytes=4 * 1024 * 1024),
    )(index, matrix)


def involution(move):
    return [(r * COLS + c, move(r, c)[0] * COLS + move(r, c)[1]) for r in range(ROWS) for c in range(COLS)]


TO_CORE = involution(lambda r, c: (r, c ^ 1))
SIDE_A = involution(lambda r, c: (r, c ^ 2 if c % 2 == 0 else c ^ 4))
SIDE_B = involution(lambda r, c: (r, c ^ 4 if c % 2 == 0 else c ^ 2))
OUTER = involution(lambda r, c: (r ^ 1, c))
MIDDLE = involution(lambda r, c: (3 - r, c) if r in (1, 2) else (r, c ^ 1))


def send(value, pairs):
    return lax.ppermute(value, AXES, pairs)


GROUPS = ((0, 1, 2, 4, 8), (3, 6, 10, 5, 9, 12), (14, 7, 11, 13), (15, 16))


def gather(a, a5):
    b = send(a, SIDE_A)
    ua = send(a5, OUTER)
    ma = send(a5, MIDDLE)
    c = send(a, SIDE_B)
    first_b = send(jnp.concatenate([b, ua[:4], ma[:4]]), SIDE_B)
    na = send(ua, MIDDLE)
    held, b = lax.optimization_barrier((ma[:4], b))
    mb = send(held, SIDE_A)
    held, ua = lax.optimization_barrier((b, ua))
    ub = send(held, OUTER)
    held, ma = lax.optimization_barrier((jnp.concatenate([a, b, c, ua, ma]), ma))
    g0 = send(held, TO_CORE)
    e = first_b[:4]
    uc = first_b[4:8]
    mc = first_b[8:]
    tile = (a5[4:] + ua[4:]) + (ma[4:] + na[4:])
    held, c = lax.optimization_barrier((ub, c))
    nb = send(held, MIDDLE)
    held, first_b = lax.optimization_barrier((e, first_b))
    ue = send(held, OUTER)
    held, na = lax.optimization_barrier((tile, na))
    tile_a = send(held, SIDE_A)
    held, mb = lax.optimization_barrier((jnp.concatenate([na[:4], tile, mb]), mb))
    second_b = send(held, SIDE_B)
    held, ub = lax.optimization_barrier((jnp.concatenate([e, uc, mc, ub, mb, na]), ub))
    g1 = send(held, TO_CORE)
    nc = second_b[:4]
    tile_b = second_b[4:5]
    me = second_b[5:]
    held, g0 = lax.optimization_barrier((jnp.concatenate([nb, tile_a]), g0))
    third_b = send(held, SIDE_B)
    ne = third_b[:4]
    tiles = jnp.concatenate([tile, tile_a, tile_b, third_b[4:]])
    held, nb = lax.optimization_barrier((jnp.concatenate([nc, ue, me, nb]), nb))
    g2 = send(held, TO_CORE)
    held, ue = lax.optimization_barrier((jnp.concatenate([ne, tiles]), ue))
    g3 = send(held, TO_CORE)
    own = (a, b, c, e, ua, ub, uc, ue, ma, mb, mc, me, na, nb, nc, ne, tiles)
    return own, (g0, g1, g2, g3)


def tile_place(big_r, delta):
    big_c = (big_r - delta) % BLOCKS
    return big_c % COLS, delta % 4, 2 * (big_c // COLS) + delta // 4


def panel_kernel(index, *refs):
    own = refs[:17]
    others = refs[17 : 17 + len(GROUPS)]
    for_me, for_next, store, extra_store, v_all, w_all, p_all, rows, acc, radii, sems = refs[17 + len(GROUPS) :]
    r, c = index[0], index[1]

    def source_of(number, col):
        z, side = number // 4, number % 4
        row = (r, r ^ 1, 3 - r, (3 - r) ^ 1)[z]
        even = lax.rem(col, 2) == 0
        flip = (0, jnp.where(even, 2, 4), jnp.where(even, 4, 2), 6)[side]
        return row, col ^ flip

    copies = []

    def load(source, start, number, col):
        row, from_col = source_of(number, col)
        d = lax.rem(row - from_col + COLS, ROWS)
        copies.append(
            pltpu.make_async_copy(source.at[pl.ds(start, 4)], store.at[from_col, d], sems.at[len(copies)])
        )

    def load_extra(source, start, col):
        for side in range(4):
            _, from_col = source_of(side, col)
            copies.append(
                pltpu.make_async_copy(source.at[start + side], extra_store.at[from_col], sems.at[len(copies)])
            )

    load_extra(own[16], 0, c)
    for ref, group in zip(others, GROUPS):
        start = 0
        for number in group:
            if number == 16:
                load_extra(ref, start, c ^ 1)
            else:
                load(ref, start, number, c ^ 1)
            start += own[number].shape[0]
    for copy in copies:
        copy.start()
    for number in range(16):
        row, from_col = source_of(number, c)
        store[from_col, lax.rem(row - from_col + COLS, ROWS)] = own[number][:4]
    for copy in copies:
        copy.wait()

    def tile(big_r, delta):
        if delta == HALF:
            return extra_store[big_r - HALF]
        return store[tile_place(big_r, delta)]

    block_row = lax.broadcasted_iota(jnp.int32, (BLOCKS, TILE), 0)
    lane = lax.broadcasted_iota(jnp.int32, (BLOCKS, TILE), 1)
    position = block_row * TILE + lane
    on_diagonal = lax.broadcasted_iota(jnp.int32, (PANEL, TILE), 0) == lax.broadcasted_iota(
        jnp.int32, (PANEL, TILE), 1
    )
    which = lax.broadcasted_iota(jnp.int32, (BLOCKS, PANEL, TILE), 1)
    which_sub = lax.broadcasted_iota(jnp.int32, (1, TILE), 1)

    def total(x):
        return jnp.sum(jnp.sum(x, axis=0, keepdims=True), axis=1, keepdims=True)

    for big_c in range(BLOCKS):
        delta = -big_c % BLOCKS
        if delta < HALF:
            rows[big_c] = tile(0, delta)[:16]
        else:
            rows[big_c] = jnp.transpose(tile(big_c, big_c))[:16]
    v_all[...] = jnp.zeros_like(v_all)
    w_all[...] = jnp.zeros_like(w_all)
    p_all[...] = rows[:, :PANEL, :]
    radii[...] = jnp.zeros_like(radii)

    def multiply(vector):
        for big_c in range(BLOCKS):
            acc[big_c] = jnp.zeros((8, TILE), jnp.float32)
        sums = []
        for big_r in range(BLOCKS):
            down = jnp.transpose(jnp.broadcast_to(vector[big_r : big_r + 1], (TILE, TILE)))
            across = None
            for delta in range(HALF + 1):
                if delta == HALF and big_r < HALF:
                    continue
                big_c = (big_r - delta) % BLOCKS
                t = tile(big_r, delta)
                acc[big_c] += jnp.sum((t * down).reshape(LANES8, 8, TILE), axis=0)
                if delta > 0:
                    part = t * vector[big_c : big_c + 1]
                    across = part if across is None else across + part
            sums.append(jnp.sum(jnp.transpose(across).reshape(LANES8, 8, TILE), axis=0))
        for big_r in range(BLOCKS):
            acc[big_r] += sums[big_r]
        return jnp.sum(acc[...], axis=1)

    def step(j, column):
        first = position == j + 1
        tail = jnp.where(position > j + 1, column, 0.0)
        tail_product = multiply(tail)
        leading = total(jnp.where(first, column, 0.0))
        squares = total(tail * tail)
        radius = jnp.sqrt(leading * leading + squares)
        denominator = leading + radius
        scaling = denominator / radius
        inverse = 1.0 / denominator
        v = jnp.where(first, 1.0, tail * inverse)
        v3 = v[:, None, :]
        refl, images = v_all[...], w_all[...]
        refl_proj = jnp.sum(jnp.sum(refl * v3, axis=0), axis=1, keepdims=True)
        image_proj = jnp.sum(jnp.sum(images * v3, axis=0), axis=1, keepdims=True)
        correction = jnp.sum(refl * image_proj[None] + images * refl_proj[None], axis=1)
        v_correction = 2.0 * jnp.sum(refl_proj * image_proj, axis=0, keepdims=True)
        product = tail_product * inverse + rows[:, pl.ds(j + 1, 1), :].reshape(BLOCKS, TILE)
        inner = scaling * (total(v * product) - v_correction)
        w = scaling * (product - correction) - (0.5 * scaling * inner) * v
        w3 = w[:, None, :]
        v_heads = jnp.sum(jnp.where(on_diagonal, v[0:1], 0.0), axis=1, keepdims=True)
        w_heads = jnp.sum(jnp.where(on_diagonal, w[0:1], 0.0), axis=1, keepdims=True)
        panel = p_all[...] - w_heads[None] * v3 - v_heads[None] * w3
        p_all[...] = panel
        v_all[...] = jnp.where(which == j, v3, refl)
        w_all[...] = jnp.where(which == j, w3, images)
        radii[...] = jnp.where(which_sub == j, -radius, radii[...])
        return jnp.sum(jnp.where(which == j + 1, panel, 0.0), axis=1)

    steps = jnp.where(jnp.logical_or(r == 1, r == 2), PANEL, 0)
    lax.fori_loop(0, steps, step, rows[:, 0, :])
    for out, row in ((for_me, r), (for_next, r ^ 1)):
        blocks = [k * ROWS + row for k in range(4)] + [m * COLS + c for m in range(2)]
        for place, number in enumerate(blocks):
            out[place, :PANEL, :] = v_all[number]
            out[place, PANEL:, :] = w_all[number]
        out[6] = jnp.broadcast_to(radii[...], (2 * PANEL, TILE))


def reduce_panel(index, own, others):
    held = pl.BlockSpec(memory_space=pltpu.VMEM)
    vmem = pl.BlockSpec(memory_space=pltpu.VMEM)
    return pl.pallas_call(
        panel_kernel,
        out_shape=(jax.ShapeDtypeStruct((7, 2 * PANEL, TILE), jnp.float32),) * 2,
        in_specs=[pl.BlockSpec(memory_space=pltpu.SMEM)] + [held] * (17 + len(others)),
        out_specs=(vmem, vmem),
        scratch_shapes=[
            pltpu.VMEM((COLS, ROWS, 4, TILE, TILE), jnp.float32),
            pltpu.VMEM((HALF, TILE, TILE), jnp.float32),
            pltpu.VMEM((BLOCKS, PANEL, TILE), jnp.float32),
            pltpu.VMEM((BLOCKS, PANEL, TILE), jnp.float32),
            pltpu.VMEM((BLOCKS, PANEL, TILE), jnp.float32),
            pltpu.VMEM((BLOCKS, 2 * PANEL, TILE), jnp.float32),
            pltpu.VMEM((BLOCKS, 8, TILE), jnp.float32),
            pltpu.VMEM((1, TILE), jnp.float32),
            pltpu.SemaphoreType.DMA((40,)),
        ],
        compiler_params=pltpu.CompilerParams(vmem_limit_bytes=24 * 1024 * 1024),
    )(index, *own, *others)


def update_kernel(index, matrix, mine, theirs, updated, refl_rows, image_rows, subdiag, held):
    r = index[0]

    @pl.when(jnp.logical_or(r == 1, r == 2))
    def _():
        held[...] = mine[...]

    @pl.when(jnp.logical_or(r == 0, r == 3))
    def _():
        held[...] = theirs[...]

    right = []
    for m in range(2):
        both = held[4 + m]
        right.append(jnp.concatenate([both[PANEL:], both[:PANEL]], axis=0))
    right = jnp.concatenate(right, axis=1)
    for k in range(4):
        left = held[k]
        span = slice(k * TILE, (k + 1) * TILE)
        updated[span, :] = matrix[span, :] - lax.dot_general(
            left,
            right,
            (((0,), (0,)), ((), ())),
            precision=lax.Precision.HIGHEST,
            preferred_element_type=jnp.float32,
        )
        refl_rows[:, span] = left[:PANEL]
        image_rows[:, span] = left[PANEL:]
    subdiag[...] = held[6, 0, :PANEL]


def finish(index, matrix, mine, theirs):
    vmem = pl.BlockSpec(memory_space=pltpu.VMEM)
    rows, _ = matrix.shape
    return pl.pallas_call(
        update_kernel,
        out_shape=(
            jax.ShapeDtypeStruct(matrix.shape, jnp.float32),
            jax.ShapeDtypeStruct((PANEL, rows), jnp.float32),
            jax.ShapeDtypeStruct((PANEL, rows), jnp.float32),
            jax.ShapeDtypeStruct((PANEL,), jnp.float32),
        ),
        in_specs=[pl.BlockSpec(memory_space=pltpu.SMEM), vmem, vmem, vmem],
        out_specs=(vmem,) * 4,
        scratch_shapes=[pltpu.VMEM(mine.shape, jnp.float32)],
        compiler_params=pltpu.CompilerParams(vmem_limit_bytes=6 * 1024 * 1024),
    )(index, matrix, mine, theirs)


def gathered(matrix):
    index = jnp.stack([lax.axis_index("row"), lax.axis_index("col")]).astype(jnp.int32)
    own, others = gather(*pick(index, matrix))
    mine, for_next = reduce_panel(index, own, others)
    return tuple(finish(index, matrix, mine, send(for_next, OUTER)))


def per_device(matrix):
    grid = (lax.axis_size("row"), lax.axis_size("col"))
    if grid == (ROWS, COLS) and matrix.shape == (BLOCKS // ROWS * TILE, BLOCKS // COLS * TILE):
        return gathered(matrix)
    return distributed(matrix)


def solution(mesh):
    return jax.shard_map(
        per_device,
        mesh=mesh,
        in_specs=(P("row", "col"),),
        out_specs=(P("row", "col"), P(None, "row"), P(None, "row"), P()),
        check_vma=False,
    )
```

```python
import jax
import jax.numpy as jnp
from jax import lax
from jax.experimental import pallas as pl
from jax.experimental.pallas import tpu as pltpu
from jax.sharding import PartitionSpec as P

TILE = 128
PANEL = 8
AXES = ("row", "col")
ROWS, COLS = 4, 8
BLOCKS = 16
HALF = BLOCKS // 2
LANES8 = TILE // 8


def everywhere(value):
    row_count, col_count = lax.axis_size("row"), lax.axis_size("col")
    spread = jnp.broadcast_to(value[None], (row_count * col_count,) + value.shape)
    got = lax.all_to_all(spread, AXES, 0, 0, tiled=False)
    return got.reshape((row_count, col_count) + value.shape)


def distributed(matrix):
    highest = lax.Precision.HIGHEST
    local_rows, local_cols = matrix.shape
    row_count, col_count = lax.axis_size("row"), lax.axis_size("col")
    grid_row, grid_col = lax.axis_index("row"), lax.axis_index("col")
    row_tiles, col_tiles = local_rows // TILE, local_cols // TILE
    order = local_rows * row_count
    position = jnp.arange(order, dtype=jnp.int32)

    def my_rows(vectors):
        shaped = vectors.reshape(vectors.shape[:-1] + (row_tiles, row_count, TILE))
        picked = lax.dynamic_index_in_dim(shaped, grid_row, axis=shaped.ndim - 2, keepdims=False)
        return picked.reshape(vectors.shape[:-1] + (local_rows,))

    def my_cols(vectors):
        shaped = vectors.reshape(vectors.shape[:-1] + (col_tiles, col_count, TILE))
        picked = lax.dynamic_index_in_dim(shaped, grid_col, axis=shaped.ndim - 2, keepdims=False)
        return picked.reshape(vectors.shape[:-1] + (local_cols,))

    def global_cols(pieces):
        shaped = pieces.reshape(pieces.shape[:-1] + (col_tiles, TILE))
        return jnp.moveaxis(shaped, 0, -2).reshape(pieces.shape[1:-1] + (order,))

    panel = global_cols(everywhere(matrix[:PANEL])[0])
    refl = jnp.zeros((PANEL, order), jnp.float32)
    images = jnp.zeros((PANEL, order), jnp.float32)
    subdiag_list = []
    for j in range(PANEL):
        column = panel[j]
        for k in range(j):
            column = column - images[k, j] * refl[k] - refl[k, j] * images[k]
        leading = column[j + 1]
        tail = jnp.where(position > j + 1, column, 0.0)
        radius = jnp.sqrt(leading * leading + jnp.sum(tail * tail))
        denominator = leading + radius
        scaling = denominator / radius
        reflector = jnp.where(position == j + 1, 1.0, tail / denominator)
        partial = jnp.sum(matrix * my_rows(reflector)[:, None], axis=0)
        product = global_cols(jnp.sum(everywhere(partial), axis=0))
        refl_proj = jnp.sum(refl * reflector, axis=1)
        image_proj = jnp.sum(images * reflector, axis=1)
        image = product
        for k in range(j):
            image = image - image_proj[k] * refl[k] - refl_proj[k] * images[k]
        image = scaling * image
        image = image - (0.5 * scaling * jnp.sum(image * reflector)) * reflector
        refl = refl.at[j].set(reflector)
        images = images.at[j].set(image)
        subdiag_list.append(-radius)
    refl_rows, image_rows = my_rows(refl), my_rows(images)
    updated = (
        matrix
        - jnp.dot(jnp.transpose(refl_rows), my_cols(images), precision=highest)
        - jnp.dot(jnp.transpose(image_rows), my_cols(refl), precision=highest)
    )
    return (updated, refl_rows, image_rows, jnp.stack(subdiag_list))


def pick_kernel(matrix, block, block_extra, sems):
    r, c = lax.axis_index("row"), lax.axis_index("col")
    d = lax.rem(r - c + COLS, ROWS)
    first = (c + d) // ROWS

    def tile(k, m):
        start = pl.multiple_of(lax.rem(k, ROWS) * TILE, TILE)
        return matrix.at[pl.ds(start, TILE), m * TILE : (m + 1) * TILE]

    copies = []
    for m in range(2):
        for s in range(2):
            copies.append(pltpu.make_async_copy(tile(first + 2 * m + s, m), block.at[2 * m + s], sems.at[2 * m + s]))
    copies.append(pltpu.make_async_copy(tile(first + 2, 0), block_extra.at[4], sems.at[4]))
    for copy in copies:
        copy.start()
    for copy in copies:
        copy.wait()
    block_extra[:4] = block[...]
    block_extra[4] = jnp.where(d == 0, block_extra[4], 0.0)


def pick(matrix):
    vmem = pl.BlockSpec(memory_space=pltpu.VMEM)
    return pl.pallas_call(
        pick_kernel,
        out_shape=(
            jax.ShapeDtypeStruct((4, TILE, TILE), jnp.float32),
            jax.ShapeDtypeStruct((5, TILE, TILE), jnp.float32),
        ),
        in_specs=[pl.BlockSpec(memory_space=pltpu.HBM)],
        out_specs=(vmem, vmem),
        scratch_shapes=[pltpu.SemaphoreType.DMA((5,))],
        compiler_params=pltpu.CompilerParams(vmem_limit_bytes=4 * 1024 * 1024),
    )(matrix)


def involution(move):
    return [(r * COLS + c, move(r, c)[0] * COLS + move(r, c)[1]) for r in range(ROWS) for c in range(COLS)]


TO_CORE = involution(lambda r, c: (r, c ^ 1))
SIDE_A = involution(lambda r, c: (r, c ^ 2 if c % 2 == 0 else c ^ 4))
SIDE_B = involution(lambda r, c: (r, c ^ 4 if c % 2 == 0 else c ^ 2))
OUTER = involution(lambda r, c: (r ^ 1, c))
MIDDLE = involution(lambda r, c: (3 - r, c) if r in (1, 2) else (r, c ^ 1))


def send(value, pairs):
    return lax.ppermute(value, AXES, pairs)


GROUPS = ((0, 1, 2, 4, 8), (3, 6, 10, 5, 9, 12), (14, 7, 11, 13), (15, 16))


def gather(a, a5):
    b = send(a, SIDE_A)
    ua = send(a5, OUTER)
    ma = send(a5, MIDDLE)
    c = send(a, SIDE_B)
    first_b = send(jnp.concatenate([b, ua[:4], ma[:4]]), SIDE_B)
    na = send(ua, MIDDLE)
    held, b = lax.optimization_barrier((ma[:4], b))
    mb = send(held, SIDE_A)
    held, ua = lax.optimization_barrier((b, ua))
    ub = send(held, OUTER)
    held, ma = lax.optimization_barrier((jnp.concatenate([a, b, c, ua, ma]), ma))
    g0 = send(held, TO_CORE)
    e = first_b[:4]
    uc = first_b[4:8]
    mc = first_b[8:]
    tile = (a5[4:] + ua[4:]) + (ma[4:] + na[4:])
    held, c = lax.optimization_barrier((ub, c))
    nb = send(held, MIDDLE)
    held, first_b = lax.optimization_barrier((e, first_b))
    ue = send(held, OUTER)
    held, na = lax.optimization_barrier((tile, na))
    tile_a = send(held, SIDE_A)
    held, mb = lax.optimization_barrier((jnp.concatenate([na[:4], tile, mb]), mb))
    second_b = send(held, SIDE_B)
    held, ub = lax.optimization_barrier((jnp.concatenate([e, uc, mc, ub, mb, na]), ub))
    g1 = send(held, TO_CORE)
    nc = second_b[:4]
    tile_b = second_b[4:5]
    me = second_b[5:]
    held, g0 = lax.optimization_barrier((jnp.concatenate([nb, tile_a]), g0))
    third_b = send(held, SIDE_B)
    ne = third_b[:4]
    tiles = jnp.concatenate([tile, tile_a, tile_b, third_b[4:]])
    held, nb = lax.optimization_barrier((jnp.concatenate([nc, ue, me, nb]), nb))
    g2 = send(held, TO_CORE)
    held, ue = lax.optimization_barrier((jnp.concatenate([ne, tiles]), ue))
    g3 = send(held, TO_CORE)
    own = (a, b, c, e, ua, ub, uc, ue, ma, mb, mc, me, na, nb, nc, ne, tiles)
    return own, (g0, g1, g2, g3)


def tile_place(big_r, delta):
    big_c = (big_r - delta) % BLOCKS
    return big_c % COLS, delta % 4, 2 * (big_c // COLS) + delta // 4


def panel_kernel(*refs):
    own = refs[:17]
    others = refs[17 : 17 + len(GROUPS)]
    for_me, for_next, store, extra_store, v_all, w_all, p_all, rows, acc, radii, sems = refs[17 + len(GROUPS) :]
    r, c = lax.axis_index("row"), lax.axis_index("col")

    def source_of(number, col):
        z, side = number // 4, number % 4
        row = (r, r ^ 1, 3 - r, (3 - r) ^ 1)[z]
        even = lax.rem(col, 2) == 0
        flip = (0, jnp.where(even, 2, 4), jnp.where(even, 4, 2), 6)[side]
        return row, col ^ flip

    copies = []

    def load(source, start, number, col):
        row, from_col = source_of(number, col)
        d = lax.rem(row - from_col + COLS, ROWS)
        copies.append(
            pltpu.make_async_copy(source.at[pl.ds(start, 4)], store.at[from_col, d], sems.at[len(copies)])
        )

    def load_extra(source, start, col):
        for side in range(4):
            _, from_col = source_of(side, col)
            copies.append(
                pltpu.make_async_copy(source.at[start + side], extra_store.at[from_col], sems.at[len(copies)])
            )

    load_extra(own[16], 0, c)
    for ref, group in zip(others, GROUPS):
        start = 0
        for number in group:
            if number == 16:
                load_extra(ref, start, c ^ 1)
            else:
                load(ref, start, number, c ^ 1)
            start += own[number].shape[0]
    for copy in copies:
        copy.start()
    for number in range(16):
        row, from_col = source_of(number, c)
        store[from_col, lax.rem(row - from_col + COLS, ROWS)] = own[number][:4]
    for copy in copies:
        copy.wait()

    def tile(big_r, delta):
        if delta == HALF:
            return extra_store[big_r - HALF]
        return store[tile_place(big_r, delta)]

    block_row = lax.broadcasted_iota(jnp.int32, (BLOCKS, TILE), 0)
    lane = lax.broadcasted_iota(jnp.int32, (BLOCKS, TILE), 1)
    position = block_row * TILE + lane
    on_diagonal = lax.broadcasted_iota(jnp.int32, (PANEL, TILE), 0) == lax.broadcasted_iota(
        jnp.int32, (PANEL, TILE), 1
    )
    which = lax.broadcasted_iota(jnp.int32, (BLOCKS, PANEL, TILE), 1)
    which_sub = lax.broadcasted_iota(jnp.int32, (1, TILE), 1)

    def total(x):
        return jnp.sum(jnp.sum(x, axis=0, keepdims=True), axis=1, keepdims=True)

    for big_c in range(BLOCKS):
        delta = -big_c % BLOCKS
        if delta < HALF:
            rows[big_c] = tile(0, delta)[:16]
        else:
            rows[big_c] = jnp.transpose(tile(big_c, big_c))[:16]
    v_all[...] = jnp.zeros_like(v_all)
    w_all[...] = jnp.zeros_like(w_all)
    p_all[...] = rows[:, :PANEL, :]
    radii[...] = jnp.zeros_like(radii)

    def multiply(vector):
        for big_c in range(BLOCKS):
            acc[big_c] = jnp.zeros((8, TILE), jnp.float32)
        sums = []
        for big_r in range(BLOCKS):
            down = jnp.transpose(jnp.broadcast_to(vector[big_r : big_r + 1], (TILE, TILE)))
            across = None
            for delta in range(HALF + 1):
                if delta == HALF and big_r < HALF:
                    continue
                big_c = (big_r - delta) % BLOCKS
                t = tile(big_r, delta)
                acc[big_c] += jnp.sum((t * down).reshape(LANES8, 8, TILE), axis=0)
                if delta > 0:
                    part = t * vector[big_c : big_c + 1]
                    across = part if across is None else across + part
            sums.append(jnp.sum(jnp.transpose(across).reshape(LANES8, 8, TILE), axis=0))
        for big_r in range(BLOCKS):
            acc[big_r] += sums[big_r]
        return jnp.sum(acc[...], axis=1)

    def step(j, column):
        first = position == j + 1
        tail = jnp.where(position > j + 1, column, 0.0)
        tail_product = multiply(tail)
        leading = total(jnp.where(first, column, 0.0))
        squares = total(tail * tail)
        radius = jnp.sqrt(leading * leading + squares)
        denominator = leading + radius
        scaling = denominator / radius
        inverse = 1.0 / denominator
        v = jnp.where(first, 1.0, tail * inverse)
        v3 = v[:, None, :]
        refl, images = v_all[...], w_all[...]
        refl_proj = jnp.sum(jnp.sum(refl * v3, axis=0), axis=1, keepdims=True)
        image_proj = jnp.sum(jnp.sum(images * v3, axis=0), axis=1, keepdims=True)
        correction = jnp.sum(refl * image_proj[None] + images * refl_proj[None], axis=1)
        v_correction = 2.0 * jnp.sum(refl_proj * image_proj, axis=0, keepdims=True)
        product = tail_product * inverse + rows[:, pl.ds(j + 1, 1), :].reshape(BLOCKS, TILE)
        inner = scaling * (total(v * product) - v_correction)
        w = scaling * (product - correction) - (0.5 * scaling * inner) * v
        w3 = w[:, None, :]
        v_heads = jnp.sum(jnp.where(on_diagonal, v[0:1], 0.0), axis=1, keepdims=True)
        w_heads = jnp.sum(jnp.where(on_diagonal, w[0:1], 0.0), axis=1, keepdims=True)
        panel = p_all[...] - w_heads[None] * v3 - v_heads[None] * w3
        p_all[...] = panel
        v_all[...] = jnp.where(which == j, v3, refl)
        w_all[...] = jnp.where(which == j, w3, images)
        radii[...] = jnp.where(which_sub == j, -radius, radii[...])
        return jnp.sum(jnp.where(which == j + 1, panel, 0.0), axis=1)

    steps = jnp.where(jnp.logical_or(r == 1, r == 2), PANEL, 0)
    lax.fori_loop(0, steps, step, rows[:, 0, :])
    for out, row in ((for_me, r), (for_next, r ^ 1)):
        blocks = [k * ROWS + row for k in range(4)] + [m * COLS + c for m in range(2)]
        for place, number in enumerate(blocks):
            out[place, :PANEL, :] = v_all[number]
            out[place, PANEL:, :] = w_all[number]
        out[6] = jnp.broadcast_to(radii[...], (2 * PANEL, TILE))


def reduce_panel(own, others):
    held = pl.BlockSpec(memory_space=pltpu.VMEM)
    vmem = pl.BlockSpec(memory_space=pltpu.VMEM)
    return pl.pallas_call(
        panel_kernel,
        out_shape=(jax.ShapeDtypeStruct((7, 2 * PANEL, TILE), jnp.float32),) * 2,
        in_specs=[held] * (17 + len(others)),
        out_specs=(vmem, vmem),
        scratch_shapes=[
            pltpu.VMEM((COLS, ROWS, 4, TILE, TILE), jnp.float32),
            pltpu.VMEM((HALF, TILE, TILE), jnp.float32),
            pltpu.VMEM((BLOCKS, PANEL, TILE), jnp.float32),
            pltpu.VMEM((BLOCKS, PANEL, TILE), jnp.float32),
            pltpu.VMEM((BLOCKS, PANEL, TILE), jnp.float32),
            pltpu.VMEM((BLOCKS, 2 * PANEL, TILE), jnp.float32),
            pltpu.VMEM((BLOCKS, 8, TILE), jnp.float32),
            pltpu.VMEM((1, TILE), jnp.float32),
            pltpu.SemaphoreType.DMA((40,)),
        ],
        compiler_params=pltpu.CompilerParams(vmem_limit_bytes=24 * 1024 * 1024),
    )(*own, *others)


def update_kernel(matrix, mine, theirs, updated, refl_rows, image_rows, subdiag, held):
    r = lax.axis_index("row")

    @pl.when(jnp.logical_or(r == 1, r == 2))
    def _():
        held[...] = mine[...]

    @pl.when(jnp.logical_or(r == 0, r == 3))
    def _():
        held[...] = theirs[...]

    right = []
    for m in range(2):
        both = held[4 + m]
        right.append(jnp.concatenate([both[PANEL:], both[:PANEL]], axis=0))
    right = jnp.concatenate(right, axis=1)
    for k in range(4):
        left = held[k]
        span = slice(k * TILE, (k + 1) * TILE)
        updated[span, :] = matrix[span, :] - lax.dot_general(
            left,
            right,
            (((0,), (0,)), ((), ())),
            precision=lax.Precision.HIGHEST,
            preferred_element_type=jnp.float32,
        )
        refl_rows[:, span] = left[:PANEL]
        image_rows[:, span] = left[PANEL:]
    subdiag[...] = held[6, 0, :PANEL]


def finish(matrix, mine, theirs):
    vmem = pl.BlockSpec(memory_space=pltpu.VMEM)
    rows, _ = matrix.shape
    return pl.pallas_call(
        update_kernel,
        out_shape=(
            jax.ShapeDtypeStruct(matrix.shape, jnp.float32),
            jax.ShapeDtypeStruct((PANEL, rows), jnp.float32),
            jax.ShapeDtypeStruct((PANEL, rows), jnp.float32),
            jax.ShapeDtypeStruct((PANEL,), jnp.float32),
        ),
        in_specs=[vmem, vmem, vmem],
        out_specs=(vmem,) * 4,
        scratch_shapes=[pltpu.VMEM(mine.shape, jnp.float32)],
        compiler_params=pltpu.CompilerParams(vmem_limit_bytes=6 * 1024 * 1024),
    )(matrix, mine, theirs)


def gathered(matrix):
    own, others = gather(*pick(matrix))
    mine, for_next = reduce_panel(own, others)
    return tuple(finish(matrix, mine, send(for_next, OUTER)))


def per_device(matrix):
    grid = (lax.axis_size("row"), lax.axis_size("col"))
    if grid == (ROWS, COLS) and matrix.shape == (BLOCKS // ROWS * TILE, BLOCKS // COLS * TILE):
        return gathered(matrix)
    return distributed(matrix)


def solution(mesh):
    return jax.shard_map(
        per_device,
        mesh=mesh,
        in_specs=(P("row", "col"),),
        out_specs=(P("row", "col"), P(None, "row"), P(None, "row"), P()),
        check_vma=False,
    )
```

```python
import jax
import jax.numpy as jnp
from jax import lax
from jax.experimental import pallas as pl
from jax.experimental.pallas import tpu as pltpu
from jax.sharding import PartitionSpec as P

TILE = 128
PANEL = 8
AXES = ("row", "col")
ROWS, COLS = 4, 8
BLOCKS = 16
HALF = BLOCKS // 2
LANES8 = TILE // 8


def everywhere(value):
    row_count, col_count = lax.axis_size("row"), lax.axis_size("col")
    spread = jnp.broadcast_to(value[None], (row_count * col_count,) + value.shape)
    got = lax.all_to_all(spread, AXES, 0, 0, tiled=False)
    return got.reshape((row_count, col_count) + value.shape)


def distributed(matrix):
    highest = lax.Precision.HIGHEST
    local_rows, local_cols = matrix.shape
    row_count, col_count = lax.axis_size("row"), lax.axis_size("col")
    grid_row, grid_col = lax.axis_index("row"), lax.axis_index("col")
    row_tiles, col_tiles = local_rows // TILE, local_cols // TILE
    order = local_rows * row_count
    position = jnp.arange(order, dtype=jnp.int32)

    def my_rows(vectors):
        shaped = vectors.reshape(vectors.shape[:-1] + (row_tiles, row_count, TILE))
        picked = lax.dynamic_index_in_dim(shaped, grid_row, axis=shaped.ndim - 2, keepdims=False)
        return picked.reshape(vectors.shape[:-1] + (local_rows,))

    def my_cols(vectors):
        shaped = vectors.reshape(vectors.shape[:-1] + (col_tiles, col_count, TILE))
        picked = lax.dynamic_index_in_dim(shaped, grid_col, axis=shaped.ndim - 2, keepdims=False)
        return picked.reshape(vectors.shape[:-1] + (local_cols,))

    def global_cols(pieces):
        shaped = pieces.reshape(pieces.shape[:-1] + (col_tiles, TILE))
        return jnp.moveaxis(shaped, 0, -2).reshape(pieces.shape[1:-1] + (order,))

    panel = global_cols(everywhere(matrix[:PANEL])[0])
    refl = jnp.zeros((PANEL, order), jnp.float32)
    images = jnp.zeros((PANEL, order), jnp.float32)
    subdiag_list = []
    for j in range(PANEL):
        column = panel[j]
        for k in range(j):
            column = column - images[k, j] * refl[k] - refl[k, j] * images[k]
        leading = column[j + 1]
        tail = jnp.where(position > j + 1, column, 0.0)
        radius = jnp.sqrt(leading * leading + jnp.sum(tail * tail))
        denominator = leading + radius
        scaling = denominator / radius
        reflector = jnp.where(position == j + 1, 1.0, tail / denominator)
        partial = jnp.sum(matrix * my_rows(reflector)[:, None], axis=0)
        product = global_cols(jnp.sum(everywhere(partial), axis=0))
        refl_proj = jnp.sum(refl * reflector, axis=1)
        image_proj = jnp.sum(images * reflector, axis=1)
        image = product
        for k in range(j):
            image = image - image_proj[k] * refl[k] - refl_proj[k] * images[k]
        image = scaling * image
        image = image - (0.5 * scaling * jnp.sum(image * reflector)) * reflector
        refl = refl.at[j].set(reflector)
        images = images.at[j].set(image)
        subdiag_list.append(-radius)
    refl_rows, image_rows = my_rows(refl), my_rows(images)
    updated = (
        matrix
        - jnp.dot(jnp.transpose(refl_rows), my_cols(images), precision=highest)
        - jnp.dot(jnp.transpose(image_rows), my_cols(refl), precision=highest)
    )
    return (updated, refl_rows, image_rows, jnp.stack(subdiag_list))


def pick_kernel(matrix, block, block_extra, sems):
    r, c = lax.axis_index("row"), lax.axis_index("col")
    d = lax.rem(r - c + COLS, ROWS)
    first = (c + d) // ROWS

    def tile(k, m):
        start = pl.multiple_of(lax.rem(k, ROWS) * TILE, TILE)
        return matrix.at[pl.ds(start, TILE), m * TILE : (m + 1) * TILE]

    copies = []
    for m in range(2):
        for s in range(2):
            copies.append(pltpu.make_async_copy(tile(first + 2 * m + s, m), block.at[2 * m + s], sems.at[2 * m + s]))
    copies.append(pltpu.make_async_copy(tile(first + 2, 0), block_extra.at[4], sems.at[4]))
    for copy in copies:
        copy.start()
    for copy in copies:
        copy.wait()
    block_extra[:4] = block[...]
    block_extra[4] = jnp.where(d == 0, block_extra[4], 0.0)


def pick(matrix):
    vmem = pl.BlockSpec(memory_space=pltpu.VMEM)
    return pl.pallas_call(
        pick_kernel,
        out_shape=(
            jax.ShapeDtypeStruct((4, TILE, TILE), jnp.float32),
            jax.ShapeDtypeStruct((5, TILE, TILE), jnp.float32),
        ),
        in_specs=[pl.BlockSpec(memory_space=pltpu.HBM)],
        out_specs=(vmem, vmem),
        scratch_shapes=[pltpu.SemaphoreType.DMA((5,))],
        compiler_params=pltpu.CompilerParams(vmem_limit_bytes=4 * 1024 * 1024),
    )(matrix)


def involution(move):
    return [(r * COLS + c, move(r, c)[0] * COLS + move(r, c)[1]) for r in range(ROWS) for c in range(COLS)]


TO_CORE = involution(lambda r, c: (r, c ^ 1))
SIDE_A = involution(lambda r, c: (r, c ^ 2 if c % 2 == 0 else c ^ 4))
SIDE_B = involution(lambda r, c: (r, c ^ 4 if c % 2 == 0 else c ^ 2))
OUTER = involution(lambda r, c: (r ^ 1, c))
MIDDLE = involution(lambda r, c: (3 - r, c) if r in (1, 2) else (r, c ^ 1))


def send(value, pairs):
    return lax.ppermute(value, AXES, pairs)


GROUPS = ((0, 1, 2, 4, 8), (3, 6, 10, 5, 9, 12), (14, 7, 11, 13), (15, 16))


def gather(a, a5):
    b = send(a, SIDE_A)
    ua = send(a5, OUTER)
    ma = send(a5, MIDDLE)
    c = send(a, SIDE_B)
    first_b = send(jnp.concatenate([b, ua[:4], ma[:4]]), SIDE_B)
    na = send(ua, MIDDLE)
    held, b = lax.optimization_barrier((ma[:4], b))
    mb = send(held, SIDE_A)
    held, ua = lax.optimization_barrier((b, ua))
    ub = send(held, OUTER)
    held, ma = lax.optimization_barrier((jnp.concatenate([a, b, c, ua, ma]), ma))
    g0 = send(held, TO_CORE)
    e = first_b[:4]
    uc = first_b[4:8]
    mc = first_b[8:]
    tile = (a5[4:] + ua[4:]) + (ma[4:] + na[4:])
    held, c = lax.optimization_barrier((ub, c))
    nb = send(held, MIDDLE)
    held, first_b = lax.optimization_barrier((e, first_b))
    ue = send(held, OUTER)
    held, na = lax.optimization_barrier((tile, na))
    tile_a = send(held, SIDE_A)
    held, mb = lax.optimization_barrier((jnp.concatenate([na[:4], tile, mb]), mb))
    second_b = send(held, SIDE_B)
    held, ub = lax.optimization_barrier((jnp.concatenate([e, uc, mc, ub, mb, na]), ub))
    g1 = send(held, TO_CORE)
    nc = second_b[:4]
    tile_b = second_b[4:5]
    me = second_b[5:]
    held, g0 = lax.optimization_barrier((jnp.concatenate([nb, tile_a]), g0))
    third_b = send(held, SIDE_B)
    ne = third_b[:4]
    tiles = jnp.concatenate([tile, tile_a, tile_b, third_b[4:]])
    held, nb = lax.optimization_barrier((jnp.concatenate([nc, ue, me, nb]), nb))
    g2 = send(held, TO_CORE)
    held, ue = lax.optimization_barrier((jnp.concatenate([ne, tiles]), ue))
    g3 = send(held, TO_CORE)
    own = (a, b, c, e, ua, ub, uc, ue, ma, mb, mc, me, na, nb, nc, ne, tiles)
    return own, (g0, g1, g2, g3)


def tile_place(big_r, delta):
    big_c = (big_r - delta) % BLOCKS
    return big_c % COLS, delta % 4, 2 * (big_c // COLS) + delta // 4


def panel_kernel(*refs):
    own = refs[:17]
    others = refs[17 : 17 + len(GROUPS)]
    for_me, for_next, store, extra_store, v_all, w_all, p_all, rows, acc, radii, sems = refs[17 + len(GROUPS) :]
    r, c = lax.axis_index("row"), lax.axis_index("col")

    def source_of(number, col):
        z, side = number // 4, number % 4
        row = (r, r ^ 1, 3 - r, (3 - r) ^ 1)[z]
        even = lax.rem(col, 2) == 0
        flip = (0, jnp.where(even, 2, 4), jnp.where(even, 4, 2), 6)[side]
        return row, col ^ flip

    copies = []

    def load(source, start, number, col):
        row, from_col = source_of(number, col)
        d = lax.rem(row - from_col + COLS, ROWS)
        copies.append(
            pltpu.make_async_copy(source.at[pl.ds(start, 4)], store.at[from_col, d], sems.at[len(copies)])
        )

    def load_extra(source, start, col):
        for side in range(4):
            _, from_col = source_of(side, col)
            copies.append(
                pltpu.make_async_copy(source.at[start + side], extra_store.at[from_col], sems.at[len(copies)])
            )

    load_extra(own[16], 0, c)
    for ref, group in zip(others, GROUPS):
        start = 0
        for number in group:
            if number == 16:
                load_extra(ref, start, c ^ 1)
            else:
                load(ref, start, number, c ^ 1)
            start += own[number].shape[0]
    for copy in copies:
        copy.start()
    for number in range(16):
        row, from_col = source_of(number, c)
        store[from_col, lax.rem(row - from_col + COLS, ROWS)] = own[number][:4]
    for copy in copies:
        copy.wait()

    def tile(big_r, delta):
        if delta == HALF:
            return extra_store[big_r - HALF]
        return store[tile_place(big_r, delta)]

    block_row = lax.broadcasted_iota(jnp.int32, (BLOCKS, TILE), 0)
    lane = lax.broadcasted_iota(jnp.int32, (BLOCKS, TILE), 1)
    position = block_row * TILE + lane
    on_diagonal = lax.broadcasted_iota(jnp.int32, (PANEL, TILE), 0) == lax.broadcasted_iota(
        jnp.int32, (PANEL, TILE), 1
    )
    which = lax.broadcasted_iota(jnp.int32, (BLOCKS, PANEL, TILE), 1)
    which_sub = lax.broadcasted_iota(jnp.int32, (1, TILE), 1)

    def total(x):
        return jnp.sum(jnp.sum(x, axis=0, keepdims=True), axis=1, keepdims=True)

    for big_c in range(BLOCKS):
        delta = -big_c % BLOCKS
        if delta < HALF:
            rows[big_c] = tile(0, delta)[:16]
        else:
            rows[big_c] = jnp.transpose(tile(big_c, big_c))[:16]
    v_all[...] = jnp.zeros_like(v_all)
    w_all[...] = jnp.zeros_like(w_all)
    p_all[...] = rows[:, :PANEL, :]
    radii[...] = jnp.zeros_like(radii)

    def multiply(vector):
        for big_c in range(BLOCKS):
            acc[big_c] = jnp.zeros((8, TILE), jnp.float32)
        sums = []
        for big_r in range(BLOCKS):
            down = jnp.transpose(jnp.broadcast_to(vector[big_r : big_r + 1], (TILE, TILE)))
            across = None
            for delta in range(HALF + 1):
                if delta == HALF and big_r < HALF:
                    continue
                big_c = (big_r - delta) % BLOCKS
                t = tile(big_r, delta)
                acc[big_c] += jnp.sum((t * down).reshape(LANES8, 8, TILE), axis=0)
                if delta > 0:
                    part = t * vector[big_c : big_c + 1]
                    across = part if across is None else across + part
            sums.append(jnp.sum(jnp.transpose(across).reshape(LANES8, 8, TILE), axis=0))
        for big_r in range(BLOCKS):
            acc[big_r] += sums[big_r]
        return jnp.sum(acc[...], axis=1)

    def step(j, column):
        first = position == j + 1
        tail = jnp.where(position > j + 1, column, 0.0)
        tail_product = multiply(tail)
        leading = total(jnp.where(first, column, 0.0))
        squares = total(tail * tail)
        radius = jnp.sqrt(leading * leading + squares)
        denominator = leading + radius
        scaling = denominator / radius
        inverse = 1.0 / denominator
        v = jnp.where(first, 1.0, tail * inverse)
        v3 = v[:, None, :]
        refl, images = v_all[...], w_all[...]
        refl_proj = jnp.sum(jnp.sum(refl * v3, axis=0), axis=1, keepdims=True)
        image_proj = jnp.sum(jnp.sum(images * v3, axis=0), axis=1, keepdims=True)
        correction = jnp.sum(refl * image_proj[None] + images * refl_proj[None], axis=1)
        v_correction = 2.0 * jnp.sum(refl_proj * image_proj, axis=0, keepdims=True)
        product = tail_product * inverse + rows[:, pl.ds(j + 1, 1), :].reshape(BLOCKS, TILE)
        inner = scaling * (total(v * product) - v_correction)
        w = scaling * (product - correction) - (0.5 * scaling * inner) * v
        ahead = p_all[:, pl.ds(jnp.minimum(j + 1, PANEL - 1), 1), :].reshape(BLOCKS, TILE)
        column = ahead - total(jnp.where(first, w, 0.0)) * v - w
        w3 = w[:, None, :]
        v_heads = jnp.sum(jnp.where(on_diagonal, v[0:1], 0.0), axis=1, keepdims=True)
        w_heads = jnp.sum(jnp.where(on_diagonal, w[0:1], 0.0), axis=1, keepdims=True)
        p_all[...] = p_all[...] - w_heads[None] * v3 - v_heads[None] * w3
        v_all[...] = jnp.where(which == j, v3, refl)
        w_all[...] = jnp.where(which == j, w3, images)
        radii[...] = jnp.where(which_sub == j, -radius, radii[...])
        return column

    steps = jnp.where(jnp.logical_or(r == 1, r == 2), PANEL, 0)
    lax.fori_loop(0, steps, step, rows[:, 0, :])
    for out, row in ((for_me, r), (for_next, r ^ 1)):
        blocks = [k * ROWS + row for k in range(4)] + [m * COLS + c for m in range(2)]
        for place, number in enumerate(blocks):
            out[place, :PANEL, :] = v_all[number]
            out[place, PANEL:, :] = w_all[number]
        out[6] = jnp.broadcast_to(radii[...], (2 * PANEL, TILE))


def reduce_panel(own, others):
    held = pl.BlockSpec(memory_space=pltpu.VMEM)
    vmem = pl.BlockSpec(memory_space=pltpu.VMEM)
    return pl.pallas_call(
        panel_kernel,
        out_shape=(jax.ShapeDtypeStruct((7, 2 * PANEL, TILE), jnp.float32),) * 2,
        in_specs=[held] * (17 + len(others)),
        out_specs=(vmem, vmem),
        scratch_shapes=[
            pltpu.VMEM((COLS, ROWS, 4, TILE, TILE), jnp.float32),
            pltpu.VMEM((HALF, TILE, TILE), jnp.float32),
            pltpu.VMEM((BLOCKS, PANEL, TILE), jnp.float32),
            pltpu.VMEM((BLOCKS, PANEL, TILE), jnp.float32),
            pltpu.VMEM((BLOCKS, PANEL, TILE), jnp.float32),
            pltpu.VMEM((BLOCKS, 2 * PANEL, TILE), jnp.float32),
            pltpu.VMEM((BLOCKS, 8, TILE), jnp.float32),
            pltpu.VMEM((1, TILE), jnp.float32),
            pltpu.SemaphoreType.DMA((40,)),
        ],
        compiler_params=pltpu.CompilerParams(vmem_limit_bytes=24 * 1024 * 1024),
    )(*own, *others)


def update_kernel(matrix, mine, theirs, updated, refl_rows, image_rows, subdiag, held):
    r = lax.axis_index("row")

    @pl.when(jnp.logical_or(r == 1, r == 2))
    def _():
        held[...] = mine[...]

    @pl.when(jnp.logical_or(r == 0, r == 3))
    def _():
        held[...] = theirs[...]

    right = []
    for m in range(2):
        both = held[4 + m]
        right.append(jnp.concatenate([both[PANEL:], both[:PANEL]], axis=0))
    right = jnp.concatenate(right, axis=1)
    for k in range(4):
        left = held[k]
        span = slice(k * TILE, (k + 1) * TILE)
        updated[span, :] = matrix[span, :] - lax.dot_general(
            left,
            right,
            (((0,), (0,)), ((), ())),
            precision=lax.Precision.HIGHEST,
            preferred_element_type=jnp.float32,
        )
        refl_rows[:, span] = left[:PANEL]
        image_rows[:, span] = left[PANEL:]
    subdiag[...] = held[6, 0, :PANEL]


def finish(matrix, mine, theirs):
    vmem = pl.BlockSpec(memory_space=pltpu.VMEM)
    rows, _ = matrix.shape
    return pl.pallas_call(
        update_kernel,
        out_shape=(
            jax.ShapeDtypeStruct(matrix.shape, jnp.float32),
            jax.ShapeDtypeStruct((PANEL, rows), jnp.float32),
            jax.ShapeDtypeStruct((PANEL, rows), jnp.float32),
            jax.ShapeDtypeStruct((PANEL,), jnp.float32),
        ),
        in_specs=[vmem, vmem, vmem],
        out_specs=(vmem,) * 4,
        scratch_shapes=[pltpu.VMEM(mine.shape, jnp.float32)],
        compiler_params=pltpu.CompilerParams(vmem_limit_bytes=6 * 1024 * 1024),
    )(matrix, mine, theirs)


def gathered(matrix):
    own, others = gather(*pick(matrix))
    mine, for_next = reduce_panel(own, others)
    return tuple(finish(matrix, mine, send(for_next, OUTER)))


def per_device(matrix):
    grid = (lax.axis_size("row"), lax.axis_size("col"))
    if grid == (ROWS, COLS) and matrix.shape == (BLOCKS // ROWS * TILE, BLOCKS // COLS * TILE):
        return gathered(matrix)
    return distributed(matrix)


def solution(mesh):
    return jax.shard_map(
        per_device,
        mesh=mesh,
        in_specs=(P("row", "col"),),
        out_specs=(P("row", "col"), P(None, "row"), P(None, "row"), P()),
        check_vma=False,
    )
```

```python
import jax
import jax.numpy as jnp
from jax import lax
from jax.experimental import pallas as pl
from jax.experimental.pallas import tpu as pltpu
from jax.sharding import PartitionSpec as P

TILE = 128
PANEL = 8
AXES = ("row", "col")
ROWS, COLS = 4, 8
BLOCKS = 16
HALF = BLOCKS // 2
LANES8 = TILE // 8


def everywhere(value):
    row_count, col_count = lax.axis_size("row"), lax.axis_size("col")
    spread = jnp.broadcast_to(value[None], (row_count * col_count,) + value.shape)
    got = lax.all_to_all(spread, AXES, 0, 0, tiled=False)
    return got.reshape((row_count, col_count) + value.shape)


def distributed(matrix):
    highest = lax.Precision.HIGHEST
    local_rows, local_cols = matrix.shape
    row_count, col_count = lax.axis_size("row"), lax.axis_size("col")
    grid_row, grid_col = lax.axis_index("row"), lax.axis_index("col")
    row_tiles, col_tiles = local_rows // TILE, local_cols // TILE
    order = local_rows * row_count
    position = jnp.arange(order, dtype=jnp.int32)

    def my_rows(vectors):
        shaped = vectors.reshape(vectors.shape[:-1] + (row_tiles, row_count, TILE))
        picked = lax.dynamic_index_in_dim(shaped, grid_row, axis=shaped.ndim - 2, keepdims=False)
        return picked.reshape(vectors.shape[:-1] + (local_rows,))

    def my_cols(vectors):
        shaped = vectors.reshape(vectors.shape[:-1] + (col_tiles, col_count, TILE))
        picked = lax.dynamic_index_in_dim(shaped, grid_col, axis=shaped.ndim - 2, keepdims=False)
        return picked.reshape(vectors.shape[:-1] + (local_cols,))

    def global_cols(pieces):
        shaped = pieces.reshape(pieces.shape[:-1] + (col_tiles, TILE))
        return jnp.moveaxis(shaped, 0, -2).reshape(pieces.shape[1:-1] + (order,))

    panel = global_cols(everywhere(matrix[:PANEL])[0])
    refl = jnp.zeros((PANEL, order), jnp.float32)
    images = jnp.zeros((PANEL, order), jnp.float32)
    subdiag_list = []
    for j in range(PANEL):
        column = panel[j]
        for k in range(j):
            column = column - images[k, j] * refl[k] - refl[k, j] * images[k]
        leading = column[j + 1]
        tail = jnp.where(position > j + 1, column, 0.0)
        radius = jnp.sqrt(leading * leading + jnp.sum(tail * tail))
        denominator = leading + radius
        scaling = denominator / radius
        reflector = jnp.where(position == j + 1, 1.0, tail / denominator)
        partial = jnp.sum(matrix * my_rows(reflector)[:, None], axis=0)
        product = global_cols(jnp.sum(everywhere(partial), axis=0))
        refl_proj = jnp.sum(refl * reflector, axis=1)
        image_proj = jnp.sum(images * reflector, axis=1)
        image = product
        for k in range(j):
            image = image - image_proj[k] * refl[k] - refl_proj[k] * images[k]
        image = scaling * image
        image = image - (0.5 * scaling * jnp.sum(image * reflector)) * reflector
        refl = refl.at[j].set(reflector)
        images = images.at[j].set(image)
        subdiag_list.append(-radius)
    refl_rows, image_rows = my_rows(refl), my_rows(images)
    updated = (
        matrix
        - jnp.dot(jnp.transpose(refl_rows), my_cols(images), precision=highest)
        - jnp.dot(jnp.transpose(image_rows), my_cols(refl), precision=highest)
    )
    return (updated, refl_rows, image_rows, jnp.stack(subdiag_list))


def pick_kernel(matrix, block, block_extra, sems):
    r, c = lax.axis_index("row"), lax.axis_index("col")
    d = lax.rem(r - c + COLS, ROWS)
    first = (c + d) // ROWS

    def tile(k, m):
        start = pl.multiple_of(lax.rem(k, ROWS) * TILE, TILE)
        return matrix.at[pl.ds(start, TILE), m * TILE : (m + 1) * TILE]

    copies = []
    for m in range(2):
        for s in range(2):
            copies.append(pltpu.make_async_copy(tile(first + 2 * m + s, m), block.at[2 * m + s], sems.at[2 * m + s]))
    copies.append(pltpu.make_async_copy(tile(first + 2, 0), block_extra.at[4], sems.at[4]))
    for copy in copies:
        copy.start()
    for copy in copies:
        copy.wait()
    block_extra[:4] = block[...]
    block_extra[4] = jnp.where(d == 0, block_extra[4], 0.0)


def pick(matrix):
    vmem = pl.BlockSpec(memory_space=pltpu.VMEM)
    return pl.pallas_call(
        pick_kernel,
        out_shape=(
            jax.ShapeDtypeStruct((4, TILE, TILE), jnp.float32),
            jax.ShapeDtypeStruct((5, TILE, TILE), jnp.float32),
        ),
        in_specs=[pl.BlockSpec(memory_space=pltpu.HBM)],
        out_specs=(vmem, vmem),
        scratch_shapes=[pltpu.SemaphoreType.DMA((5,))],
        compiler_params=pltpu.CompilerParams(vmem_limit_bytes=4 * 1024 * 1024),
    )(matrix)


def involution(move):
    return [(r * COLS + c, move(r, c)[0] * COLS + move(r, c)[1]) for r in range(ROWS) for c in range(COLS)]


TO_CORE = involution(lambda r, c: (r, c ^ 1))
SIDE_A = involution(lambda r, c: (r, c ^ 2 if c % 2 == 0 else c ^ 4))
SIDE_B = involution(lambda r, c: (r, c ^ 4 if c % 2 == 0 else c ^ 2))
OUTER = involution(lambda r, c: (r ^ 1, c))
MIDDLE = involution(lambda r, c: (3 - r, c) if r in (1, 2) else (r, c ^ 1))


def send(value, pairs):
    return lax.ppermute(value, AXES, pairs)


GROUPS = ((0, 1, 2, 4, 8), (3, 6, 10, 5, 9, 12), (14, 7, 11, 13), (15, 16))


def gather(a, a5):
    b = send(a, SIDE_A)
    ua = send(a5, OUTER)
    ma = send(a5, MIDDLE)
    c = send(a, SIDE_B)
    first_b = send(jnp.concatenate([b, ua[:4], ma[:4]]), SIDE_B)
    held, c = lax.optimization_barrier((ua, c))
    na = send(held, MIDDLE)
    held, b = lax.optimization_barrier((ma[:4], b))
    mb = send(held, SIDE_A)
    held, ma = lax.optimization_barrier((b, ma))
    ub = send(held, OUTER)
    held, ma = lax.optimization_barrier((jnp.concatenate([a, b, c, ua, ma]), ma))
    g0 = send(held, TO_CORE)
    e = first_b[:4]
    uc = first_b[4:8]
    mc = first_b[8:]
    tile = (a5[4:] + ua[4:]) + (ma[4:] + na[4:])
    held, c = lax.optimization_barrier((ub, c))
    nb = send(held, MIDDLE)
    held, first_b = lax.optimization_barrier((e, first_b))
    ue = send(held, OUTER)
    held, na = lax.optimization_barrier((tile, na))
    tile_a = send(held, SIDE_A)
    held, mb = lax.optimization_barrier((jnp.concatenate([na[:4], tile, mb]), mb))
    second_b = send(held, SIDE_B)
    held, ub = lax.optimization_barrier((jnp.concatenate([e, uc, mc, ub, mb, na]), ub))
    g1 = send(held, TO_CORE)
    nc = second_b[:4]
    tile_b = second_b[4:5]
    me = second_b[5:]
    held, g0 = lax.optimization_barrier((jnp.concatenate([nb, tile_a]), g0))
    third_b = send(held, SIDE_B)
    ne = third_b[:4]
    tiles = jnp.concatenate([tile, tile_a, tile_b, third_b[4:]])
    held, nb = lax.optimization_barrier((jnp.concatenate([nc, ue, me, nb]), nb))
    g2 = send(held, TO_CORE)
    held, ue = lax.optimization_barrier((jnp.concatenate([ne, tiles]), ue))
    g3 = send(held, TO_CORE)
    own = (a, b, c, e, ua, ub, uc, ue, ma, mb, mc, me, na, nb, nc, ne, tiles)
    return own, (g0, g1, g2, g3)


def tile_place(big_r, delta):
    big_c = (big_r - delta) % BLOCKS
    return big_c % COLS, delta % 4, 2 * (big_c // COLS) + delta // 4


def panel_kernel(*refs):
    own = refs[:17]
    others = refs[17 : 17 + len(GROUPS)]
    for_me, for_next, store, extra_store, v_all, w_all, p_all, rows, acc, radii, sems = refs[17 + len(GROUPS) :]
    r, c = lax.axis_index("row"), lax.axis_index("col")

    def source_of(number, col):
        z, side = number // 4, number % 4
        row = (r, r ^ 1, 3 - r, (3 - r) ^ 1)[z]
        even = lax.rem(col, 2) == 0
        flip = (0, jnp.where(even, 2, 4), jnp.where(even, 4, 2), 6)[side]
        return row, col ^ flip

    copies = []

    def load(source, start, number, col):
        row, from_col = source_of(number, col)
        d = lax.rem(row - from_col + COLS, ROWS)
        copies.append(
            pltpu.make_async_copy(source.at[pl.ds(start, 4)], store.at[from_col, d], sems.at[len(copies)])
        )

    def load_extra(source, start, col):
        for side in range(4):
            _, from_col = source_of(side, col)
            copies.append(
                pltpu.make_async_copy(source.at[start + side], extra_store.at[from_col], sems.at[len(copies)])
            )

    load_extra(own[16], 0, c)
    for ref, group in zip(others, GROUPS):
        start = 0
        for number in group:
            if number == 16:
                load_extra(ref, start, c ^ 1)
            else:
                load(ref, start, number, c ^ 1)
            start += own[number].shape[0]
    for copy in copies:
        copy.start()
    for number in range(16):
        row, from_col = source_of(number, c)
        store[from_col, lax.rem(row - from_col + COLS, ROWS)] = own[number][:4]
    for copy in copies:
        copy.wait()

    def tile(big_r, delta):
        if delta == HALF:
            return extra_store[big_r - HALF]
        return store[tile_place(big_r, delta)]

    block_row = lax.broadcasted_iota(jnp.int32, (BLOCKS, TILE), 0)
    lane = lax.broadcasted_iota(jnp.int32, (BLOCKS, TILE), 1)
    position = block_row * TILE + lane
    on_diagonal = lax.broadcasted_iota(jnp.int32, (PANEL, TILE), 0) == lax.broadcasted_iota(
        jnp.int32, (PANEL, TILE), 1
    )
    which = lax.broadcasted_iota(jnp.int32, (BLOCKS, PANEL, TILE), 1)
    which_sub = lax.broadcasted_iota(jnp.int32, (1, TILE), 1)

    def total(x):
        return jnp.sum(jnp.sum(x, axis=0, keepdims=True), axis=1, keepdims=True)

    for big_c in range(BLOCKS):
        delta = -big_c % BLOCKS
        if delta < HALF:
            rows[big_c] = tile(0, delta)[:16]
        else:
            rows[big_c] = jnp.transpose(tile(big_c, big_c))[:16]
    v_all[...] = jnp.zeros_like(v_all)
    w_all[...] = jnp.zeros_like(w_all)
    p_all[...] = rows[:, :PANEL, :]
    radii[...] = jnp.zeros_like(radii)

    def multiply(vector):
        for big_c in range(BLOCKS):
            acc[big_c] = jnp.zeros((8, TILE), jnp.float32)
        sums = []
        for big_r in range(BLOCKS):
            down = jnp.transpose(jnp.broadcast_to(vector[big_r : big_r + 1], (TILE, TILE)))
            across = None
            for delta in range(HALF + 1):
                if delta == HALF and big_r < HALF:
                    continue
                big_c = (big_r - delta) % BLOCKS
                t = tile(big_r, delta)
                acc[big_c] += jnp.sum((t * down).reshape(LANES8, 8, TILE), axis=0)
                if delta > 0:
                    part = t * vector[big_c : big_c + 1]
                    across = part if across is None else across + part
            sums.append(jnp.sum(jnp.transpose(across).reshape(LANES8, 8, TILE), axis=0))
        for big_r in range(BLOCKS):
            acc[big_r] += sums[big_r]
        return jnp.sum(acc[...], axis=1)

    def step(j, column):
        first = position == j + 1
        tail = jnp.where(position > j + 1, column, 0.0)
        tail_product = multiply(tail)
        leading = total(jnp.where(first, column, 0.0))
        squares = total(tail * tail)
        radius = jnp.sqrt(leading * leading + squares)
        denominator = leading + radius
        scaling = denominator / radius
        inverse = 1.0 / denominator
        v = jnp.where(first, 1.0, tail * inverse)
        v3 = v[:, None, :]
        refl, images = v_all[...], w_all[...]
        refl_proj = jnp.sum(jnp.sum(refl * v3, axis=0), axis=1, keepdims=True)
        image_proj = jnp.sum(jnp.sum(images * v3, axis=0), axis=1, keepdims=True)
        correction = jnp.sum(refl * image_proj[None] + images * refl_proj[None], axis=1)
        v_correction = 2.0 * jnp.sum(refl_proj * image_proj, axis=0, keepdims=True)
        product = tail_product * inverse + rows[:, pl.ds(j + 1, 1), :].reshape(BLOCKS, TILE)
        inner = scaling * (total(v * product) - v_correction)
        w = scaling * (product - correction) - (0.5 * scaling * inner) * v
        ahead = p_all[:, pl.ds(jnp.minimum(j + 1, PANEL - 1), 1), :].reshape(BLOCKS, TILE)
        column = ahead - total(jnp.where(first, w, 0.0)) * v - w
        w3 = w[:, None, :]
        v_heads = jnp.sum(jnp.where(on_diagonal, v[0:1], 0.0), axis=1, keepdims=True)
        w_heads = jnp.sum(jnp.where(on_diagonal, w[0:1], 0.0), axis=1, keepdims=True)
        p_all[...] = p_all[...] - w_heads[None] * v3 - v_heads[None] * w3
        v_all[...] = jnp.where(which == j, v3, refl)
        w_all[...] = jnp.where(which == j, w3, images)
        radii[...] = jnp.where(which_sub == j, -radius, radii[...])
        return column

    steps = jnp.where(jnp.logical_or(r == 1, r == 2), PANEL, 0)
    lax.fori_loop(0, steps, step, rows[:, 0, :])
    for out, row in ((for_me, r), (for_next, r ^ 1)):
        blocks = [k * ROWS + row for k in range(4)] + [m * COLS + c for m in range(2)]
        for place, number in enumerate(blocks):
            out[place, :PANEL, :] = v_all[number]
            out[place, PANEL:, :] = w_all[number]
        out[6] = jnp.broadcast_to(radii[...], (2 * PANEL, TILE))


def reduce_panel(own, others):
    held = pl.BlockSpec(memory_space=pltpu.VMEM)
    vmem = pl.BlockSpec(memory_space=pltpu.VMEM)
    return pl.pallas_call(
        panel_kernel,
        out_shape=(jax.ShapeDtypeStruct((7, 2 * PANEL, TILE), jnp.float32),) * 2,
        in_specs=[held] * (17 + len(others)),
        out_specs=(vmem, vmem),
        scratch_shapes=[
            pltpu.VMEM((COLS, ROWS, 4, TILE, TILE), jnp.float32),
            pltpu.VMEM((HALF, TILE, TILE), jnp.float32),
            pltpu.VMEM((BLOCKS, PANEL, TILE), jnp.float32),
            pltpu.VMEM((BLOCKS, PANEL, TILE), jnp.float32),
            pltpu.VMEM((BLOCKS, PANEL, TILE), jnp.float32),
            pltpu.VMEM((BLOCKS, 2 * PANEL, TILE), jnp.float32),
            pltpu.VMEM((BLOCKS, 8, TILE), jnp.float32),
            pltpu.VMEM((1, TILE), jnp.float32),
            pltpu.SemaphoreType.DMA((40,)),
        ],
        compiler_params=pltpu.CompilerParams(vmem_limit_bytes=24 * 1024 * 1024),
    )(*own, *others)


def update_kernel(matrix, mine, theirs, updated, refl_rows, image_rows, subdiag, held):
    r = lax.axis_index("row")

    @pl.when(jnp.logical_or(r == 1, r == 2))
    def _():
        held[...] = mine[...]

    @pl.when(jnp.logical_or(r == 0, r == 3))
    def _():
        held[...] = theirs[...]

    right = []
    for m in range(2):
        both = held[4 + m]
        right.append(jnp.concatenate([both[PANEL:], both[:PANEL]], axis=0))
    right = jnp.concatenate(right, axis=1)
    for k in range(4):
        left = held[k]
        span = slice(k * TILE, (k + 1) * TILE)
        updated[span, :] = matrix[span, :] - lax.dot_general(
            left,
            right,
            (((0,), (0,)), ((), ())),
            precision=lax.Precision.HIGHEST,
            preferred_element_type=jnp.float32,
        )
        refl_rows[:, span] = left[:PANEL]
        image_rows[:, span] = left[PANEL:]
    subdiag[...] = held[6, 0, :PANEL]


def finish(matrix, mine, theirs):
    vmem = pl.BlockSpec(memory_space=pltpu.VMEM)
    rows, _ = matrix.shape
    return pl.pallas_call(
        update_kernel,
        out_shape=(
            jax.ShapeDtypeStruct(matrix.shape, jnp.float32),
            jax.ShapeDtypeStruct((PANEL, rows), jnp.float32),
            jax.ShapeDtypeStruct((PANEL, rows), jnp.float32),
            jax.ShapeDtypeStruct((PANEL,), jnp.float32),
        ),
        in_specs=[vmem, vmem, vmem],
        out_specs=(vmem,) * 4,
        scratch_shapes=[pltpu.VMEM(mine.shape, jnp.float32)],
        compiler_params=pltpu.CompilerParams(vmem_limit_bytes=6 * 1024 * 1024),
    )(matrix, mine, theirs)


def gathered(matrix):
    own, others = gather(*pick(matrix))
    mine, for_next = reduce_panel(own, others)
    return tuple(finish(matrix, mine, send(for_next, OUTER)))


def per_device(matrix):
    grid = (lax.axis_size("row"), lax.axis_size("col"))
    if grid == (ROWS, COLS) and matrix.shape == (BLOCKS // ROWS * TILE, BLOCKS // COLS * TILE):
        return gathered(matrix)
    return distributed(matrix)


def solution(mesh):
    return jax.shard_map(
        per_device,
        mesh=mesh,
        in_specs=(P("row", "col"),),
        out_specs=(P("row", "col"), P(None, "row"), P(None, "row"), P()),
        check_vma=False,
    )
```
